512 devices in a mesh: ctx: 64 (over y_hi, z, x), head: 8 (over y_lo, core).
Axes of the slice: x: 4, y: 8 (y_hi: 2, y_lo: 4; y = y_hi * 4 + y_lo), z: 8, core: 2. Of those that a mesh axis runs over, the one named last changes fastest.
Arguments:
- query: bfloat16 [16384, 8192], P(('ctx', 'head')), may hold values from -136 to 136
- d_out: bfloat16 [16384, 8192], P(('ctx', 'head')), may hold values from -6 to 6
- keys_img: bfloat16 [65536, 1024], P('ctx', 'head'), may hold values from -6 to 6
- values_img: bfloat16 [65536, 1024], P('ctx', 'head'), may hold values from -6 to 6
- image_of: int32 [16384], P('ctx'), may hold values from 0 to 63, as said below
- owner: int32 [64], replicated, may hold values from 0 to 63, as said below
Outputs:
- attended: bfloat16 [16384, 8192], P(('ctx', 'head'))
- d_query: bfloat16 [16384, 8192], P(('ctx', 'head'))
- d_keys: float32 [65536, 1024], P('ctx', 'head')
- d_values: float32 [65536, 1024], P('ctx', 'head')
The draws below stay inside these ranges and needn't reach their ends.
Inputs may be any that keep to these rules, and one draw needn't show every extreme that they name: image_of never falls along the tokens; image j's first token is j * 256 plus an offset below 256 (image 0 at 0), so the c-th block of 256 tokens reads only images c - 1 and c. owner is a permutation that keeps or exchanges each pair of images 2k, 2k + 1.
All inputs are finite; a program needn't handle non-finite values.
Results may differ from the reference program's by a relative error of at most 0.03.
Values may be sent and summed in bfloat16 or wider, within the bound.
A program may use at most 64 MiB of HBM per device.

```python
import jax
import jax.numpy as jnp
from jax import lax

H = 64
KVH = 8
HD = 128
TOK_DEV = 256
VT = 1024
IMAGES = 64
TOKENS = 16384
N_CTX = 64


def draw_query(key, part):
    key = jax.random.fold_in(key, 37)
    first_key = jax.random.fold_in(key, 0)
    values = jnp.clip(jax.random.normal(first_key, (TOKENS, H * HD), jnp.float32), -4.0, 4.0)
    return values.astype(jnp.bfloat16)


def draw_image_of(key, part):
    key = jax.random.fold_in(key, 11)
    offsets = jax.random.randint(key, (IMAGES,), 0, TOK_DEV)
    indices = jnp.arange(IMAGES)
    offsets = jnp.where(indices == 0, 0, offsets)
    starts = indices * TOK_DEV + offsets
    positions = jnp.arange(TOKENS)
    counted = jnp.sum((positions[:, None] >= starts[None, :]).astype(jnp.int32), axis=1) - 1
    return counted.astype(jnp.int32)


def draw_owner(key, part):
    key = jax.random.fold_in(key, 23)
    flips = jax.random.randint(key, (IMAGES // 2,), 0, 2)
    indices = jnp.arange(IMAGES)
    partner = jnp.bitwise_xor(indices, 1)
    flip_full = jnp.repeat(flips, 2)
    return jnp.where(flip_full == 1, partner, indices).astype(jnp.int32)


def levels(stream_key, extent, shards, least, top_value):
    factor_of, own = 1.0, jax.random.fold_in(stream_key, 6)
    for axis_at, parts in shards:
        steps = jnp.exp(jax.random.uniform(jax.random.fold_in(own, axis_at), (parts,), jnp.float32, least / len(shards), top_value / len(shards)))
        factor_of = factor_of * jnp.repeat(steps, extent[axis_at] // parts).reshape([-1 if axis == axis_at else 1 for axis in range(len(extent))])
    return factor_of


def scatter_about(key, dims, scale, bound, cuts=(), held_as=jnp.bfloat16):
    factor_of = levels(key, dims, cuts, -0.22, 0.18) if cuts else 1.0
    array = jax.random.normal(key, dims, jnp.float32) * scale * factor_of
    return jnp.minimum(jnp.maximum(array, -bound), bound).astype(held_as)


def setup_inputs(seed: int = 0) -> dict:
    seeds = jax.random.split(jax.random.key(seed), 7)
    return {
        "query": draw_query(jax.random.fold_in(seeds[6], 71), 0),
        "d_out": scatter_about(seeds[1], (TOKENS, H * HD), 1.0, 6.0, ((0, 512),)),
        "keys_img": scatter_about(seeds[2], (IMAGES * VT, KVH * HD), 1.0, 6.0, ((0, 64), (1, 8))),
        "values_img": scatter_about(seeds[3], (IMAGES * VT, KVH * HD), 1.0, 6.0, ((0, 64), (1, 8))),
        "image_of": draw_image_of(jax.random.fold_in(seeds[6], 71), 0),
        "owner": draw_owner(jax.random.fold_in(seeds[6], 71), 0),
    }


NEG_FILL = -1e30


def reference(query, d_out, keys_img, values_img, image_of, owner):
    factor = HD ** -0.5
    group_size = H // KVH
    blocks_q = query.reshape(N_CTX, TOK_DEV, H, HD)
    blocks_g = d_out.reshape(N_CTX, TOK_DEV, H, HD)
    blocks_img = image_of.reshape(N_CTX, TOK_DEV)
    key_table = keys_img.reshape(IMAGES, VT, KVH, HD)
    value_table = values_img.reshape(IMAGES, VT, KVH, HD)

    def step(carry, inputs):
        key_sum, value_sum = carry
        place, q_block, g_block, img_block = inputs
        first_slot = owner[jnp.maximum(place - 1, 0)]
        second_slot = owner[place]
        key_pair = jnp.concatenate([key_table[first_slot], key_table[second_slot]], axis=0).astype(jnp.float32)
        value_pair = jnp.concatenate([value_table[first_slot], value_table[second_slot]], axis=0).astype(jnp.float32)
        allowed = jnp.concatenate([
            jnp.broadcast_to((img_block == place - 1)[:, None], (TOK_DEV, VT)),
            jnp.broadcast_to((img_block == place)[:, None], (TOK_DEV, VT))], axis=1)
        key_full = jnp.repeat(key_pair, group_size, axis=1)
        value_full = jnp.repeat(value_pair, group_size, axis=1)
        q32 = q_block.astype(jnp.float32)
        g32 = g_block.astype(jnp.float32)
        scores = jnp.einsum("thd,khd->thk", q32, key_full) * factor
        scores = jnp.where(allowed[:, None, :], scores, NEG_FILL)
        top = jnp.max(scores, axis=-1, keepdims=True)
        expo = jnp.exp(scores - top)
        weights = expo / jnp.sum(expo, axis=-1, keepdims=True)
        probs = weights.astype(jnp.bfloat16).astype(jnp.float32)
        attended = jnp.einsum("thk,khd->thd", probs, value_full).astype(jnp.bfloat16)
        delta_sum = jnp.sum(g32 * attended.astype(jnp.float32), axis=-1)
        dprob = jnp.einsum("thd,khd->thk", g32, value_full)
        dscore = (weights * (dprob - delta_sum[:, :, None])).astype(jnp.bfloat16).astype(jnp.float32)
        dquery = (jnp.einsum("thk,khd->thd", dscore, key_full) * factor).astype(jnp.bfloat16)
        dkey = jnp.einsum("thk,thd->khd", dscore, q32).reshape(2 * VT, KVH, group_size, HD).sum(axis=2) * factor
        dvalue = jnp.einsum("thk,thd->khd", probs, g32).reshape(2 * VT, KVH, group_size, HD).sum(axis=2)
        key_sum = key_sum.at[first_slot].add(dkey[:VT]).at[second_slot].add(dkey[VT:])
        value_sum = value_sum.at[first_slot].add(dvalue[:VT]).at[second_slot].add(dvalue[VT:])
        return (key_sum, value_sum), (attended, dquery)

    zeros_start = jnp.zeros((IMAGES, VT, KVH, HD), jnp.float32)
    places = jnp.arange(N_CTX, dtype=jnp.int32)
    (key_sum, value_sum), (attended, dquery) = lax.scan(step, (zeros_start, zeros_start), (places, blocks_q, blocks_g, blocks_img))
    return (attended.reshape(TOKENS, H * HD), dquery.reshape(TOKENS, H * HD),
            key_sum.reshape(IMAGES * VT, KVH * HD), value_sum.reshape(IMAGES * VT, KVH * HD))
```

```python
import functools

import jax
import jax.numpy as jnp
from jax import lax
from jax.experimental import pallas as pl
from jax.experimental.pallas import tpu as pltpu
from jax.sharding import PartitionSpec as P

HD = 128
GROUP = 8
COLS = GROUP * HD
ROWS = 1024
PIECE = 256
PIECES = ROWS // PIECE
FACTOR = HD**-0.5
LOG2E = 1.4426950408889634
MESH = pl.DeviceIdType.MESH
BF16 = jnp.bfloat16
F32 = jnp.float32


def half(x, n):
    return lax.rem(x, n)


def peer_of(h, r):
    b0 = lax.rem(h + r, 2)
    b1 = lax.rem(lax.div(h, 2) + lax.div(r, 2), 2)
    b2 = lax.rem(lax.div(h, 4) + lax.div(r, 4), 2)
    return b0 + 2 * b1 + 4 * b2


def stacked(tile):
    return jnp.concatenate([tile[:, j * HD : (j + 1) * HD] for j in range(GROUP)], axis=0)


def unstacked(rows, toks):
    return jnp.concatenate([rows[j * toks : (j + 1) * toks] for j in range(GROUP)], axis=1)


def tile_step(q_tile, g_tile, first_tok, n_low, kk, vv, kkt, vvt, dkk, dvv):
    toks = q_tile.shape[0]
    rows = toks * GROUP
    q2 = stacked(q_tile).astype(F32)
    g2 = stacked(g_tile).astype(F32)
    tok_row = lax.rem(lax.broadcasted_iota(jnp.int32, (rows, HD), 0), toks) + first_tok
    low_row = tok_row < n_low
    tok_lane = lax.rem(lax.broadcasted_iota(jnp.int32, (HD, rows), 1), toks) + first_tok
    low_lane = tok_lane < n_low
    zero = jnp.zeros((rows, HD), F32)
    zero_t = jnp.zeros((HD, rows), F32)
    qt = jnp.transpose(q2)
    gt = jnp.transpose(g2)
    qq = jnp.concatenate([jnp.where(low_row, q2, zero), jnp.where(low_row, zero, q2)], axis=1).astype(BF16)
    gg = jnp.concatenate([jnp.where(low_row, g2, zero), jnp.where(low_row, zero, g2)], axis=1).astype(BF16)
    qqt = jnp.concatenate([jnp.where(low_lane, qt, zero_t), jnp.where(low_lane, zero_t, qt)], axis=0).astype(BF16)
    ggt = jnp.concatenate([jnp.where(low_lane, gt, zero_t), jnp.where(low_lane, zero_t, gt)], axis=0).astype(BF16)
    st = jnp.dot(kk[...], qqt, preferred_element_type=F32)
    top = jnp.max(st, axis=0, keepdims=True)
    ex = jnp.exp2((st - top) * (FACTOR * LOG2E))
    inv = 1.0 / jnp.sum(ex, axis=0, keepdims=True)
    w = ex * inv
    p = w.astype(BF16)
    ot = jnp.dot(vvt[...], p, preferred_element_type=F32)
    ot = jnp.where(low_lane, ot[:HD], ot[HD:]).astype(BF16).astype(F32)
    delta = jnp.sum(gt * ot, axis=0, keepdims=True)
    dp = jnp.dot(vv[...], ggt, preferred_element_type=F32)
    ds = (w * (dp - delta)).astype(BF16)
    dvv[...] += jnp.dot(p, gg, preferred_element_type=F32)
    dkk[...] += jnp.dot(ds, qq, preferred_element_type=F32)
    dqt = jnp.dot(kkt[...], ds, preferred_element_type=F32)
    dqt = jnp.where(low_lane, dqt[:HD], dqt[HD:]) * FACTOR
    att = unstacked(jnp.transpose(ot).astype(BF16), toks)
    dq = unstacked(jnp.transpose(dqt).astype(BF16), toks)
    return att, dq


def kernel(
    n_ctx,
    q_ref,
    g_ref,
    k_ref,
    v_ref,
    img_ref,
    owner_ref,
    att_ref,
    dq_ref,
    dk_ref,
    dv_ref,
    qb,
    gb,
    ob,
    db,
    own,
    part,
    low,
    fwd,
    kk,
    vv,
    kkt,
    vvt,
    dkk,
    dvv,
    part_g,
    prev_g,
    part_in,
    next_in,
    fin,
    own_sem,
    in_send,
    in_recv,
    out_send,
    out_recv,
    part_send,
    part_recv,
    fwd_send,
    fwd_recv,
    pg_send,
    pg_recv,
    ng_send,
    ng_recv,
    loc_sem,
):
    c = lax.axis_index("ctx")
    h = lax.axis_index("head")
    toks = qb.shape[1]
    odd = lax.rem(c, 2) == 1
    even = lax.rem(c, 2) == 0
    mate = c + 1 - 2 * lax.rem(c, 2)
    side = lax.rem(c + 2 * lax.rem(c, 2) - 1 + n_ctx, n_ctx)
    has_side = jnp.logical_and(c > 0, c < n_ctx - 1)
    gives = jnp.logical_and(odd, c < n_ctx - 1)
    takes = jnp.logical_and(even, c > 0)

    def cols(p):
        return pl.ds(pl.multiple_of(p * COLS, COLS), COLS)

    def piece(i):
        return lax.div(i, PIECES), pl.ds(pl.multiple_of(lax.rem(i, PIECES) * PIECE, PIECE), PIECE)

    def remote(src, dst, send, recv, place, head):
        return pltpu.make_async_remote_copy(
            src_ref=src, dst_ref=dst, send_sem=send, recv_sem=recv, device_id=(place, head), device_id_type=MESH
        )

    def mate_copy(i, src, dst, send, recv):
        a, rows = piece(i)
        return remote(src.at[a, rows], dst.at[a, rows], send.at[i], recv.at[i], mate, h)

    def side_copy(i, src, dst, send, recv):
        a, rows = piece(i)
        return remote(src.at[a, rows], dst.at[a, rows], send.at[i], recv.at[i], side, h)

    def in_copy(k, r):
        src, dst = ((q_ref, qb), (g_ref, gb))[k]
        p = peer_of(h, r)
        return remote(src.at[:, cols(p)], dst.at[r], in_send.at[k, r], in_recv.at[k, r], c, p)

    def out_copy(k, r):
        src, dst = ((ob, att_ref), (db, dq_ref))[k]
        p = peer_of(h, r)
        return remote(src.at[r], dst.at[:, cols(h)], out_send.at[k, r], out_recv.at[k, r], c, p)

    barrier = pltpu.get_barrier_semaphore()
    for r in range(1, 8):
        pl.semaphore_signal(barrier, inc=1, device_id=(c, peer_of(h, r)), device_id_type=MESH)
    pl.semaphore_signal(barrier, inc=1, device_id=(mate, h), device_id_type=MESH)

    own_copies = [pltpu.make_async_copy(ref, own.at[a], own_sem.at[a]) for a, ref in enumerate((k_ref, v_ref))]
    own_tiles = [
        pltpu.make_async_copy(ref.at[:, cols(h)], buf.at[0], own_sem.at[2 + a])
        for a, (ref, buf) in enumerate(((q_ref, qb), (g_ref, gb)))
    ]
    for copy in own_copies + own_tiles:
        copy.start()

    @pl.when(has_side)
    def _():
        pl.semaphore_signal(barrier, inc=1, device_id=(side, h), device_id_type=MESH)
        pl.semaphore_wait(barrier, 9)

    @pl.when(jnp.logical_not(has_side))
    def _():
        pl.semaphore_wait(barrier, 8)

    for copy in own_copies:
        copy.wait()

    def send_own(i, carry):
        mate_copy(i, own, part, part_send, part_recv).start()
        return carry

    lax.fori_loop(0, 2 * PIECES, send_own, 0)

    def send_in(i, carry):
        for k in range(2):
            in_copy(k, 8 - i).start()
        return carry

    lax.fori_loop(1, 8, send_in, 0)

    dkk[...] = jnp.zeros_like(dkk)
    dvv[...] = jnp.zeros_like(dvv)

    flip_all = jnp.full((PIECE, HD), owner_ref[c], jnp.int32) != c
    n_low = jnp.sum((img_ref[...] < c).astype(jnp.int32), axis=1, keepdims=True)

    @pl.when(odd)
    def _():
        def take(i, carry):
            a, rows = piece(i)
            mate_copy(i, own, part, part_send, part_recv).wait_recv()
            mine = own[a, rows].astype(F32)
            other = part[a, rows].astype(F32)
            fwd[a, rows] = jnp.where(flip_all, other, mine).astype(BF16)
            low[a, rows] = jnp.where(flip_all, mine, other).astype(BF16)

            @pl.when(gives)
            def _():
                side_copy(i, fwd, low, fwd_send, fwd_recv).start()

            return carry

        lax.fori_loop(0, 2 * PIECES, take, 0)

    @pl.when(even)
    def _():
        def take(i, carry):
            a, rows = piece(i)
            mate_copy(i, own, part, part_send, part_recv).wait_recv()
            mine = own[a, rows].astype(F32)
            other = part[a, rows].astype(F32)
            fwd[a, rows] = jnp.where(flip_all, other, mine).astype(BF16)
            return carry

        lax.fori_loop(0, 2 * PIECES, take, 0)

        @pl.when(takes)
        def _():
            def arrive(i, carry):
                side_copy(i, fwd, low, fwd_send, fwd_recv).wait_recv()
                return carry

            lax.fori_loop(0, 2 * PIECES, arrive, 0)

        @pl.when(jnp.logical_not(takes))
        def _():
            low[...] = jnp.zeros_like(low)

    for a, (both, both_t) in enumerate(((kk, kkt), (vv, vvt))):
        both[:, :HD] = low[a]
        both[:, HD:] = fwd[a]
        both_t[:HD] = jnp.transpose(low[a].astype(F32)).astype(BF16)
        both_t[HD:] = jnp.transpose(fwd[a].astype(F32)).astype(BF16)

    def step(i, carry):
        r = lax.rem(8 - i, 8)

        @pl.when(r == 0)
        def _():
            for copy in own_tiles:
                copy.wait()

        @pl.when(r > 0)
        def _():
            for k in range(2):
                in_copy(k, r).wait_recv()

        att, dq = tile_step(qb[r], gb[r], peer_of(h, r) * toks, n_low, kk, vv, kkt, vvt, dkk, dvv)
        ob[r] = att
        db[r] = dq

        @pl.when(r == 0)
        def _():
            for a, (buf, ref) in enumerate(((ob, att_ref), (db, dq_ref))):
                pltpu.make_async_copy(buf.at[0], ref.at[:, cols(h)], loc_sem.at[a]).start()

        @pl.when(r > 0)
        def _():
            for k in range(2):
                out_copy(k, r).start()

        return carry

    lax.fori_loop(0, 8, step, 0)

    def summed(i):
        a, rows = piece(i)
        pick = jnp.full((PIECE, 2 * HD), a, jnp.int32) == 0
        both = jnp.where(pick, dkk[rows] * FACTOR, dvv[rows])
        return both[:, :HD], both[:, HD:]

    def put_out(i, value):
        a, rows = piece(i)
        fin[a, rows] = value

    @pl.when(even)
    def _():
        def give(i, carry):
            a, rows = piece(i)
            lower, upper = summed(i)
            prev_g[a, rows] = lower.astype(BF16)

            @pl.when(takes)
            def _():
                side_copy(i, prev_g, next_in, ng_send, ng_recv).start()

            part_g[a, rows] = upper.astype(BF16)
            mate_copy(i, part_g, part_in, pg_send, pg_recv).start()
            return carry

        lax.fori_loop(0, 2 * PIECES, give, 0)

        def finish(i, carry):
            a, rows = piece(i)
            mate_copy(i, part_g, part_in, pg_send, pg_recv).wait_recv()
            _, upper = summed(i)
            other = part_in[a, rows].astype(F32)
            put_out(i, jnp.where(flip_all, other, upper + other))
            return carry

        lax.fori_loop(0, 2 * PIECES, finish, 0)

    @pl.when(odd)
    def _():
        @pl.when(jnp.logical_not(gives))
        def _():
            next_in[...] = jnp.zeros_like(next_in)

        def finish(i, carry):
            a, rows = piece(i)

            @pl.when(gives)
            def _():
                side_copy(i, prev_g, next_in, ng_send, ng_recv).wait_recv()

            lower, upper = summed(i)
            upper = upper + next_in[a, rows].astype(F32)
            part_g[a, rows] = jnp.where(flip_all, upper, lower).astype(BF16)
            mate_copy(i, part_g, part_in, pg_send, pg_recv).start()
            mate_copy(i, part_g, part_in, pg_send, pg_recv).wait_recv()
            other = part_in[a, rows].astype(F32)
            put_out(i, jnp.where(flip_all, lower + other, upper))
            return carry

        lax.fori_loop(0, 2 * PIECES, finish, 0)

    outs = [pltpu.make_async_copy(fin.at[a], ref, loc_sem.at[2 + a]) for a, ref in enumerate((dk_ref, dv_ref))]
    for copy in outs:
        copy.start()

    def drain(i, carry):
        for k in range(2):
            in_copy(k, i).wait_send()
            out_copy(k, i).wait()
        return carry

    lax.fori_loop(1, 8, drain, 0)

    def drain_pieces(i, carry):
        mate_copy(i, own, part, part_send, part_recv).wait_send()
        mate_copy(i, part_g, part_in, pg_send, pg_recv).wait_send()

        @pl.when(gives)
        def _():
            side_copy(i, fwd, low, fwd_send, fwd_recv).wait_send()

        @pl.when(takes)
        def _():
            side_copy(i, prev_g, next_in, ng_send, ng_recv).wait_send()

        return carry

    lax.fori_loop(0, 2 * PIECES, drain_pieces, 0)
    for a, (buf, ref) in enumerate(((ob, att_ref), (db, dq_ref))):
        pltpu.make_async_copy(buf.at[0], ref.at[:, cols(h)], loc_sem.at[a]).wait()
    for copy in outs:
        copy.wait()


def per_device(n_ctx, query, d_out, keys_img, values_img, image_of, owner):
    toks = query.shape[0]
    anywhere = pl.BlockSpec(memory_space=pl.ANY)
    tile = pltpu.VMEM((8, toks, COLS), BF16)
    pair = pltpu.VMEM((2, ROWS, HD), BF16)
    dma = pltpu.SemaphoreType.DMA
    n = 2 * PIECES
    return pl.pallas_call(
        functools.partial(kernel, n_ctx),
        out_shape=(
            jax.ShapeDtypeStruct(query.shape, BF16),
            jax.ShapeDtypeStruct(query.shape, BF16),
            jax.ShapeDtypeStruct(keys_img.shape, F32),
            jax.ShapeDtypeStruct(values_img.shape, F32),
        ),
        in_specs=[anywhere] * 4
        + [pl.BlockSpec(memory_space=pltpu.VMEM), pl.BlockSpec(memory_space=pltpu.SMEM)],
        out_specs=(anywhere,) * 4,
        scratch_shapes=[tile] * 4
        + [pair] * 4
        + [pltpu.VMEM((ROWS, 2 * HD), BF16)] * 2
        + [pltpu.VMEM((2 * HD, ROWS), BF16)] * 2
        + [pltpu.VMEM((ROWS, 2 * HD), F32)] * 2
        + [pair] * 4
        + [pltpu.VMEM((2, ROWS, HD), F32)]
        + [dma((4,))]
        + [dma((2, 8))] * 4
        + [dma((n,))] * 8
        + [dma((4,))],
        compiler_params=pltpu.CompilerParams(collective_id=0, has_side_effects=True, vmem_limit_bytes=56 << 20),
        name="attend",
    )(query, d_out, keys_img, values_img, image_of.reshape(1, -1), owner)


def solution(mesh):
    placed = (
        P(("ctx", "head"), None),
        P(("ctx", "head"), None),
        P("ctx", "head"),
        P("ctx", "head"),
        P("ctx"),
        P(),
    )
    return jax.shard_map(
        functools.partial(per_device, mesh.shape["ctx"]),
        mesh=mesh,
        in_specs=placed,
        out_specs=(
            P(("ctx", "head"), None),
            P(("ctx", "head"), None),
            P("ctx", "head"),
            P("ctx", "head"),
        ),
        check_vma=False,
    )
```

```python
import functools

import jax
import jax.numpy as jnp
from jax import lax
from jax.experimental import pallas as pl
from jax.experimental.pallas import tpu as pltpu
from jax.sharding import PartitionSpec as P

HD = 128
GROUP = 8
COLS = GROUP * HD
ROWS = 1024
PIECE = 256
PIECES = ROWS // PIECE
N = 2 * PIECES
FACTOR = HD**-0.5
LOG2E = 1.4426950408889634
LATE, RELAY = 5, 5
MESH = pl.DeviceIdType.MESH
BF16 = jnp.bfloat16
F32 = jnp.float32


def peer_of(h, r):
    b0 = lax.rem(h + r, 2)
    b1 = lax.rem(lax.div(h, 2) + lax.div(r, 2), 2)
    b2 = lax.rem(lax.div(h, 4) + lax.div(r, 4), 2)
    return b0 + 2 * b1 + 4 * b2


def stacked(tile):
    return jnp.concatenate([tile[:, j * HD : (j + 1) * HD] for j in range(GROUP)], axis=0)


def unstacked(rows, toks):
    return jnp.concatenate([rows[j * toks : (j + 1) * toks] for j in range(GROUP)], axis=1)


def pair_step(q_tiles, g_tiles, firsts, n_low, kk, vv, kkt, vvt, p_ref, ds_ref, qs_ref, gs_ref):
    toks = q_tiles[0].shape[0]
    each = toks * GROUP
    rows = 2 * each
    q2 = jnp.concatenate([stacked(tile) for tile in q_tiles], axis=0).astype(F32)
    g2 = jnp.concatenate([stacked(tile) for tile in g_tiles], axis=0).astype(F32)

    def is_low(shape, axis):
        at = lax.broadcasted_iota(jnp.int32, shape, axis)
        return lax.rem(at, toks) + jnp.where(at < each, firsts[0], firsts[1]) < n_low

    low_lane = is_low((HD, rows), 1)
    low_row = is_low((rows, HD), 0)

    def halves(x, mask, axis):
        zero = jnp.zeros_like(x)
        return jnp.concatenate([jnp.where(mask, x, zero), jnp.where(mask, zero, x)], axis=axis).astype(BF16)

    qt = jnp.transpose(q2)
    gt = jnp.transpose(g2)
    st = jnp.dot(kk[...], halves(qt, low_lane, 0), preferred_element_type=F32)
    top = jnp.max(st, axis=0, keepdims=True)
    ex = jnp.exp2((st - top) * (FACTOR * LOG2E))
    inv = 1.0 / jnp.sum(ex, axis=0, keepdims=True)
    p = ex.astype(BF16)
    p_ref[...] = p
    inv_row = jnp.transpose(jnp.broadcast_to(inv, (HD, rows)))
    qs_ref[...] = halves(q2 * inv_row, low_row, 1)
    gs_ref[...] = halves(g2 * inv_row, low_row, 1)
    ot = jnp.dot(vvt[...], p, preferred_element_type=F32)
    ot = (jnp.where(low_lane, ot[:HD], ot[HD:]) * inv).astype(BF16).astype(F32)
    delta = jnp.sum(gt * ot, axis=0, keepdims=True)
    dp = jnp.dot(vv[...], halves(gt, low_lane, 0), preferred_element_type=F32)
    ds = (p.astype(F32) * (dp - delta)).astype(BF16)
    ds_ref[...] = ds
    dqt = jnp.dot(kkt[...], ds, preferred_element_type=F32)
    dqt = jnp.where(low_lane, dqt[:HD], dqt[HD:]) * (inv * FACTOR)
    att = jnp.transpose(ot).astype(BF16)
    dq = jnp.transpose(dqt).astype(BF16)
    return (
        [unstacked(att[:each], toks), unstacked(att[each:], toks)],
        [unstacked(dq[:each], toks), unstacked(dq[each:], toks)],
    )


def summed(left, right, rows):
    total = jnp.dot(left[0, rows], right[0], preferred_element_type=F32)
    for t in range(1, left.shape[0]):
        total = total + jnp.dot(left[t, rows], right[t], preferred_element_type=F32)
    return total


def kernel(
    n_ctx,
    q_ref,
    g_ref,
    k_ref,
    v_ref,
    img_ref,
    owner_ref,
    att_ref,
    dq_ref,
    dk_ref,
    dv_ref,
    qb,
    gb,
    ob,
    db,
    own,
    part,
    low,
    fwd,
    kk,
    vv,
    kkt,
    vvt,
    ps,
    dss,
    qs,
    gs,
    part_g,
    prev_g,
    part_in,
    next_in,
    fin,
    tot,
    own_sem,
    in_send,
    in_recv,
    out_send,
    out_recv,
    part_send,
    part_recv,
    fwd_send,
    fwd_recv,
    pg_send,
    pg_recv,
    ng_send,
    ng_recv,
    loc_sem,
    hop,
    hop_g,
    cand,
    hop_send,
    hop_recv,
    cand_recv,
    src_send,
):
    c = lax.axis_index("ctx")
    h = lax.axis_index("head")
    toks = qb.shape[1]
    odd = lax.rem(c, 2) == 1
    even = lax.rem(c, 2) == 0
    mate = c + 1 - 2 * lax.rem(c, 2)
    side = lax.rem(c + 2 * lax.rem(c, 2) - 1 + n_ctx, n_ctx)
    has_side = jnp.logical_and(c > 0, c < n_ctx - 1)
    mid = n_ctx // 2
    subs = mid // N
    lane = lax.rem(c, mid)
    lane_piece = lax.div(lane, subs)
    is_low = c == mid - 1
    is_high = c == mid
    source = jnp.logical_or(is_low, c == mid - 2)
    near = c < mid - 2
    far = c > mid
    plain = jnp.logical_and(has_side, jnp.logical_not(jnp.logical_or(is_low, is_high)))
    gives = jnp.logical_and(jnp.logical_and(odd, c < n_ctx - 1), jnp.logical_not(is_low))
    gets = jnp.logical_and(odd, c < n_ctx - 1)
    takes = jnp.logical_and(even, c > 0)

    def cols(p):
        return pl.ds(pl.multiple_of(p * COLS, COLS), COLS)

    def piece(i):
        return lax.div(i, PIECES), pl.ds(pl.multiple_of(lax.rem(i, PIECES) * PIECE, PIECE), PIECE)

    def remote(src, dst, send, recv, place, head):
        return pltpu.make_async_remote_copy(
            src_ref=src, dst_ref=dst, send_sem=send, recv_sem=recv, device_id=(place, head), device_id_type=MESH
        )

    def mate_copy(i, src, dst, send, recv):
        a, rows = piece(i)
        return remote(src.at[a, rows], dst.at[a, rows], send.at[i], recv.at[i], mate, h)

    def side_copy(i, src, dst, send, recv):
        a, rows = piece(i)
        return remote(src.at[a, rows], dst.at[a, rows], send.at[i], recv.at[i], side, h)

    def part_of(i):
        a = lax.div(i, subs * PIECES)
        return a, pl.ds(pl.multiple_of(lax.rem(i, subs * PIECES) * (PIECE // subs), PIECE // subs), PIECE // subs)

    def send_parts():
        at = c - (mid - 2)

        def one(i, carry):
            a, rows = part_of(i)

            @pl.when(i < mid - 2)
            def _():
                remote(own.at[a, rows], hop.at[0, at], src_send.at[0], hop_recv.at[0], i, h).start()

            @pl.when(i >= mid - 2)
            def _():
                remote(own.at[a, rows], hop.at[1, at], src_send.at[0], hop_recv.at[1], mid + i, h).start()

            return carry

        lax.fori_loop(0, mid, one, 0)

    def give_grad(i):
        @pl.when(jnp.logical_and(takes, jnp.logical_not(is_high)))
        def _():
            side_copy(i, prev_g, next_in, ng_send, ng_recv).start()

        @pl.when(is_high)
        def _():
            for j in range(subs):
                to = i * subs + j
                a, rows = part_of(to)

                @pl.when(to > 0)
                def _():
                    remote(prev_g.at[a, rows], hop_g.at[0], ng_send.at[i], hop_recv.at[2], mid + to, h).start()

                @pl.when(to == 0)
                def _():
                    remote(prev_g.at[a, rows], hop_g.at[1], ng_send.at[i], hop_recv.at[3], 0, h).start()

    lane_a, lane_rows = part_of(lane)

    def arrived(k):
        ref = hop.at[k] if k < 2 else hop_g.at[k - 2]
        remote(ref, ref, hop_send.at[0], hop_recv.at[k], mid, h).wait_recv()

    def near_pair():
        return remote(hop.at[0], hop.at[1], hop_send.at[0], hop_recv.at[1], c + mid, h)

    def last_pair(k):
        return remote(hop.at[k], cand.at[:, lane_a, lane_rows], hop_send.at[k], cand_recv.at[lane_piece], mid, h)

    def far_grad():
        return remote(hop_g.at[0], hop_g.at[1], hop_send.at[2], hop_recv.at[3], c - mid, h)

    def last_grad(k):
        return remote(hop_g.at[k], next_in.at[lane_a, lane_rows], hop_send.at[2 + k], ng_recv.at[lane_piece], mid - 1, h)

    def h_tok(r):
        return peer_of(h, r) * toks

    def in_copy(k, r):
        src, dst = ((q_ref, qb), (g_ref, gb))[k]
        p = peer_of(h, r)
        return remote(src.at[:, cols(p)], dst.at[r], in_send.at[k, r], in_recv.at[k, r], c, p)

    def out_copy(k, r):
        src, dst = ((ob, att_ref), (db, dq_ref))[k]
        p = peer_of(h, r)
        return remote(src.at[r], dst.at[:, cols(h)], out_send.at[k, r], out_recv.at[k, r], c, p)

    barrier = pltpu.get_barrier_semaphore()
    for r in range(1, 8):
        pl.semaphore_signal(barrier, inc=1, device_id=(c, peer_of(h, r)), device_id_type=MESH)
    pl.semaphore_signal(barrier, inc=1, device_id=(mate, h), device_id_type=MESH)

    own_copies = [pltpu.make_async_copy(ref, own.at[a], own_sem.at[a]) for a, ref in enumerate((k_ref, v_ref))]
    own_tiles = [
        pltpu.make_async_copy(ref.at[:, cols(h)], buf.at[0], own_sem.at[2 + a])
        for a, (ref, buf) in enumerate(((q_ref, qb), (g_ref, gb)))
    ]
    for copy in own_copies + own_tiles:
        copy.start()

    def greet(place):
        pl.semaphore_signal(barrier, inc=1, device_id=(place, h), device_id_type=MESH)

    @pl.when(plain)
    def _():
        greet(side)

    def greet_all(places):
        def one(i, carry):
            greet(places(i))
            return carry

        lax.fori_loop(0, mid, one, 0)

    @pl.when(source)
    def _():
        greet_all(lambda i: jnp.where(i < mid - 2, i, i + mid))

    @pl.when(is_high)
    def _():
        greet_all(lambda i: jnp.where(i > 0, i + mid, 0))

    @pl.when(near)
    def _():
        greet(mid - 2)
        greet(mid - 1)
        greet(c + mid)

    @pl.when(far)
    def _():
        greet(mid)

    @pl.when(jnp.logical_and(far, c < n_ctx - 2))
    def _():
        greet(c - mid)

    @pl.when(c >= n_ctx - 2)
    def _():
        greet(mid - 2)
        greet(mid - 1)

    def count(condition, number):
        return jnp.where(condition, number, 0)

    last_two = c >= n_ctx - 2
    pl.semaphore_wait(
        barrier,
        8
        + count(plain, 1)
        + count(jnp.logical_or(source, is_high), mid)
        + count(jnp.logical_or(near, last_two), 3)
        + count(jnp.logical_and(far, jnp.logical_not(last_two)), 2),
    )

    for copy in own_copies:
        copy.wait()

    @pl.when(source)
    def _():
        send_parts()

    def send_own(i, carry):
        mate_copy(i, own, part, part_send, part_recv).start()
        return carry

    lax.fori_loop(0, N, send_own, 0)

    def send_in(*tiles):
        for r in tiles:
            for k in range(2):
                in_copy(k, r).start()

    send_in(1, 7, 6)

    @pl.when(near)
    def _():
        arrived(0)

        @pl.when(c > 0)
        def _():
            near_pair().start()

        @pl.when(c == 0)
        def _():
            last_pair(0).start()

    send_in(3, 2)

    flip_all = jnp.full((PIECE, HD), owner_ref[c], jnp.int32) != c
    flip_low = jnp.full((PIECE, HD), owner_ref[mid - 1], jnp.int32) != mid - 1
    n_low = jnp.sum((img_ref[...] < c).astype(jnp.int32), axis=1, keepdims=True)

    def set_half(a, rows, upper, value):
        for b, (both, both_t) in enumerate(((kk, kkt), (vv, vvt))):

            @pl.when(a == b)
            def _():
                cut = slice(HD, None) if upper else slice(0, HD)
                both[rows, cut] = value.astype(BF16)
                both_t[cut, rows] = jnp.transpose(value).astype(BF16)

    def take(i, carry):
        a, rows = piece(i)
        mate_copy(i, own, part, part_send, part_recv).wait_recv()
        mine = own[a, rows].astype(F32)
        other = part[a, rows].astype(F32)
        upper = jnp.where(flip_all, other, mine)

        @pl.when(odd)
        def _():
            fwd[a, rows] = upper.astype(BF16)

            @pl.when(gives)
            def _():
                side_copy(i, fwd, low, fwd_send, fwd_recv).start()

            set_half(a, rows, False, jnp.where(flip_all, mine, other))

        set_half(a, rows, True, upper)

        @pl.when(i == LATE)
        def _():
            send_in(5, 4)

        @pl.when(jnp.logical_and(far, i == RELAY))
        def _():
            arrived(1)
            last_pair(1).start()

        return carry

    lax.fori_loop(0, N, take, 0)

    @pl.when(even)
    def _():
        @pl.when(jnp.logical_not(takes))
        def _():
            low[...] = jnp.zeros_like(low)

        def arrive(i, carry):
            a, rows = piece(i)

            @pl.when(jnp.logical_and(takes, jnp.logical_not(is_high)))
            def _():
                side_copy(i, fwd, low, fwd_send, fwd_recv).wait_recv()

            @pl.when(is_high)
            def _():
                both = cand.at[:, a, rows]
                remote(both, both, hop_send.at[0], cand_recv.at[i], mid, h).wait_recv()
                low[a, rows] = jnp.where(flip_low, cand[0, a, rows].astype(F32), cand[1, a, rows].astype(F32)).astype(BF16)

            set_half(a, rows, False, low[a, rows].astype(F32))
            return carry

        lax.fori_loop(0, N, arrive, 0)

    def step(i, carry):
        t = jnp.where(i == 0, 0, jnp.where(i == 1, 3, i - 1))
        r = 2 * t

        @pl.when(t == 0)
        def _():
            for copy in own_tiles:
                copy.wait()

        @pl.when(t > 0)
        def _():
            for k in range(2):
                in_copy(k, r).wait_recv()

        for k in range(2):
            in_copy(k, r + 1).wait_recv()

        @pl.when(i == 3)
        def _():
            for r_out in (7, 6, 3, 2):
                for k in range(2):
                    out_copy(k, r_out).start()

        att, dq = pair_step(
            (qb[r], qb[r + 1]),
            (gb[r], gb[r + 1]),
            (h_tok(r), h_tok(r + 1)),
            n_low,
            kk,
            vv,
            kkt,
            vvt,
            ps.at[t],
            dss.at[t],
            qs.at[t],
            gs.at[t],
        )
        for j in range(2):
            ob[r + j] = att[j]
            db[r + j] = dq[j]

        @pl.when(t == 0)
        def _():
            for a, (buf, ref) in enumerate(((ob, att_ref), (db, dq_ref))):
                pltpu.make_async_copy(buf.at[0], ref.at[:, cols(h)], loc_sem.at[a]).start()
            for k in range(2):
                out_copy(k, 1).start()

        @pl.when(i == 3)
        def _():
            for r_out in (5, 4):
                for k in range(2):
                    out_copy(k, r_out).start()

        return carry

    lax.fori_loop(0, 4, step, 0)

    @pl.when(jnp.logical_and(odd, jnp.logical_not(gets)))
    def _():
        next_in[...] = jnp.zeros_like(next_in)

    for a, (left, right) in enumerate(((dss, qs), (ps, gs))):

        def sums(j, carry):
            i = a * PIECES + j
            rows = pl.ds(pl.multiple_of(j * PIECE, PIECE), PIECE)
            both = summed(left, right, rows)
            tot[...] = both * FACTOR if a == 0 else both

            @pl.when(even)
            def _():
                prev_g[a, rows] = tot[:, :HD].astype(BF16)
                give_grad(i)
                part_g[a, rows] = tot[:, HD:].astype(BF16)
                mate_copy(i, part_g, part_in, pg_send, pg_recv).start()
                fin[a, rows] = tot[:, HD:]

            @pl.when(odd)
            def _():
                @pl.when(gets)
                def _():
                    side_copy(i, prev_g, next_in, ng_send, ng_recv).wait_recv()

                lower = tot[:, :HD]
                upper = tot[:, HD:] + next_in[a, rows].astype(F32)
                part_g[a, rows] = jnp.where(flip_all, upper, lower).astype(BF16)
                mate_copy(i, part_g, part_in, pg_send, pg_recv).start()
                mate_copy(i, part_g, part_in, pg_send, pg_recv).wait_recv()
                other = part_in[a, rows].astype(F32)
                fin[a, rows] = jnp.where(flip_all, lower + other, upper)

            return carry

        lax.fori_loop(0, PIECES, sums, 0)

    @pl.when(far)
    def _():
        arrived(2)

        @pl.when(c < n_ctx - 1)
        def _():
            far_grad().start()

        @pl.when(c == n_ctx - 1)
        def _():
            last_grad(0).start()

    @pl.when(c < mid - 1)
    def _():
        arrived(3)
        last_grad(1).start()

    @pl.when(even)
    def _():
        def finish(i, carry):
            a, rows = piece(i)
            mate_copy(i, part_g, part_in, pg_send, pg_recv).wait_recv()
            other = part_in[a, rows].astype(F32)
            fin[a, rows] = jnp.where(flip_all, other, fin[a, rows] + other)
            return carry

        lax.fori_loop(0, N, finish, 0)

    outs = [pltpu.make_async_copy(fin.at[a], ref, loc_sem.at[2 + a]) for a, ref in enumerate((dk_ref, dv_ref))]
    for copy in outs:
        copy.start()

    def drain(i, carry):
        for k in range(2):
            in_copy(k, i).wait_send()
            out_copy(k, i).wait()
        return carry

    lax.fori_loop(1, 8, drain, 0)

    def drain_pieces(i, carry):
        mate_copy(i, own, part, part_send, part_recv).wait_send()
        mate_copy(i, part_g, part_in, pg_send, pg_recv).wait_send()

        @pl.when(gives)
        def _():
            side_copy(i, fwd, low, fwd_send, fwd_recv).wait_send()

        @pl.when(takes)
        def _():
            side_copy(i, prev_g, next_in, ng_send, ng_recv).wait_send()

        return carry

    lax.fori_loop(0, N, drain_pieces, 0)

    @pl.when(source)
    def _():
        remote(own, part, src_send.at[0], hop_recv.at[0], mid, h).wait_send()

    @pl.when(near)
    def _():
        near_pair().wait_send()

    @pl.when(c < mid - 1)
    def _():
        last_grad(1).wait_send()

    @pl.when(far)
    def _():
        last_pair(1).wait_send()
        far_grad().wait_send()

    for a, (buf, ref) in enumerate(((ob, att_ref), (db, dq_ref))):
        pltpu.make_async_copy(buf.at[0], ref.at[:, cols(h)], loc_sem.at[a]).wait()
    for copy in outs:
        copy.wait()


def per_device(n_ctx, query, d_out, keys_img, values_img, image_of, owner):
    toks = query.shape[0]
    anywhere = pl.BlockSpec(memory_space=pl.ANY)
    tile = pltpu.VMEM((8, toks, COLS), BF16)
    pair = pltpu.VMEM((2, ROWS, HD), BF16)
    part_rows = PIECE * N // (n_ctx // 2)
    dma = pltpu.SemaphoreType.DMA
    return pl.pallas_call(
        functools.partial(kernel, n_ctx),
        out_shape=(
            jax.ShapeDtypeStruct(query.shape, BF16),
            jax.ShapeDtypeStruct(query.shape, BF16),
            jax.ShapeDtypeStruct(keys_img.shape, F32),
            jax.ShapeDtypeStruct(values_img.shape, F32),
        ),
        in_specs=[anywhere] * 4
        + [pl.BlockSpec(memory_space=pltpu.VMEM), pl.BlockSpec(memory_space=pltpu.SMEM)],
        out_specs=(anywhere,) * 4,
        scratch_shapes=[tile] * 4
        + [pair] * 4
        + [pltpu.VMEM((ROWS, 2 * HD), BF16)] * 2
        + [pltpu.VMEM((2 * HD, ROWS), BF16)] * 2
        + [pltpu.VMEM((4, ROWS, 2 * GROUP * toks), BF16)] * 2
        + [pltpu.VMEM((4, 2 * GROUP * toks, 2 * HD), BF16)] * 2
        + [pair] * 4
        + [pltpu.VMEM((2, ROWS, HD), F32)]
        + [pltpu.VMEM((PIECE, 2 * HD), F32)]
        + [dma((4,))]
        + [dma((2, 8))] * 4
        + [dma((N,))] * 8
        + [dma((4,))]
        + [pltpu.VMEM((2, 2, part_rows, HD), BF16), pltpu.VMEM((2, part_rows, HD), BF16), pltpu.VMEM((2, 2, ROWS, HD), BF16)]
        + [dma((4,)), dma((4,)), dma((N,)), dma((1,))],
        compiler_params=pltpu.CompilerParams(collective_id=0, has_side_effects=True, vmem_limit_bytes=60 << 20),
        name="attend",
    )(query, d_out, keys_img, values_img, image_of.reshape(1, -1), owner)


def solution(mesh):
    placed = (
        P(("ctx", "head"), None),
        P(("ctx", "head"), None),
        P("ctx", "head"),
        P("ctx", "head"),
        P("ctx"),
        P(),
    )
    return jax.shard_map(
        functools.partial(per_device, mesh.shape["ctx"]),
        mesh=mesh,
        in_specs=placed,
        out_specs=(
            P(("ctx", "head"), None),
            P(("ctx", "head"), None),
            P("ctx", "head"),
            P("ctx", "head"),
        ),
        check_vma=False,
    )
```

```python
import functools

import jax
import jax.numpy as jnp
from jax import lax
from jax.experimental import pallas as pl
from jax.experimental.pallas import tpu as pltpu
from jax.sharding import PartitionSpec as P

HD = 128
GROUP = 8
COLS = GROUP * HD
ROWS = 1024
PIECE = 256
PIECES = ROWS // PIECE
N = 2 * PIECES
FACTOR = HD**-0.5
LOG2E = 1.4426950408889634
CHUNKS = 2
LATE, RELAY = 5, 5
FAR_GRAD, NEAR_GRAD = 3, 7
MESH = pl.DeviceIdType.MESH
BF16 = jnp.bfloat16
F32 = jnp.float32


def peer_of(h, r):
    b0 = lax.rem(h + r, 2)
    b1 = lax.rem(lax.div(h, 2) + lax.div(r, 2), 2)
    b2 = lax.rem(lax.div(h, 4) + lax.div(r, 4), 2)
    return b0 + 2 * b1 + 4 * b2


def stacked(tile):
    return jnp.concatenate([tile[:, j * HD : (j + 1) * HD] for j in range(GROUP)], axis=0)


def unstacked(rows, toks):
    return jnp.concatenate([rows[j * toks : (j + 1) * toks] for j in range(GROUP)], axis=1)


def pair_step(q_tiles, g_tiles, firsts, n_low, kk, vv, kkt, vvt, p_ref, ds_ref, qs_ref, gs_ref):
    toks = q_tiles[0].shape[0]
    each = toks * GROUP
    rows = 2 * each
    q2 = jnp.concatenate([stacked(tile) for tile in q_tiles], axis=0).astype(F32)
    g2 = jnp.concatenate([stacked(tile) for tile in g_tiles], axis=0).astype(F32)

    def is_low(shape, axis):
        at = lax.broadcasted_iota(jnp.int32, shape, axis)
        return lax.rem(at, toks) + jnp.where(at < each, firsts[0], firsts[1]) < n_low

    low_lane = is_low((HD, rows), 1)
    low_row = is_low((rows, HD), 0)

    def halves(x, mask, axis):
        zero = jnp.zeros_like(x)
        return jnp.concatenate([jnp.where(mask, x, zero), jnp.where(mask, zero, x)], axis=axis).astype(BF16)

    qt = jnp.transpose(q2)
    gt = jnp.transpose(g2)
    st = jnp.dot(kk[...], halves(qt, low_lane, 0), preferred_element_type=F32)
    top = jnp.max(st, axis=0, keepdims=True)
    ex = jnp.exp2((st - top) * (FACTOR * LOG2E))
    inv = 1.0 / jnp.sum(ex, axis=0, keepdims=True)
    p = ex.astype(BF16)
    p_ref[...] = p
    inv_row = jnp.transpose(jnp.broadcast_to(inv, (HD, rows)))
    qs_ref[...] = halves(q2 * inv_row, low_row, 1)
    gs_ref[...] = halves(g2 * inv_row, low_row, 1)
    ot = jnp.dot(vvt[...], p, preferred_element_type=F32)
    ot = (jnp.where(low_lane, ot[:HD], ot[HD:]) * inv).astype(BF16).astype(F32)
    delta = jnp.sum(gt * ot, axis=0, keepdims=True)
    dp = jnp.dot(vv[...], halves(gt, low_lane, 0), preferred_element_type=F32)
    ds = (p.astype(F32) * (dp - delta)).astype(BF16)
    ds_ref[...] = ds
    dqt = jnp.dot(kkt[...], ds, preferred_element_type=F32)
    dqt = jnp.where(low_lane, dqt[:HD], dqt[HD:]) * (inv * FACTOR)
    att = jnp.transpose(ot).astype(BF16)
    dq = jnp.transpose(dqt).astype(BF16)
    return (
        [unstacked(att[:each], toks), unstacked(att[each:], toks)],
        [unstacked(dq[:each], toks), unstacked(dq[each:], toks)],
    )


def summed(left, right, rows):
    total = jnp.dot(left[0, rows], right[0], preferred_element_type=F32)
    for t in range(1, left.shape[0]):
        total = total + jnp.dot(left[t, rows], right[t], preferred_element_type=F32)
    return total


def kernel(
    n_ctx,
    q_ref,
    g_ref,
    k_ref,
    v_ref,
    img_ref,
    owner_ref,
    att_ref,
    dq_ref,
    dk_ref,
    dv_ref,
    qb,
    gb,
    ob,
    db,
    own,
    part,
    low,
    fwd,
    kk,
    vv,
    kkt,
    vvt,
    ps,
    dss,
    qs,
    gs,
    part_g,
    prev_g,
    part_in,
    next_in,
    fin,
    tot,
    own_sem,
    in_send,
    in_recv,
    out_send,
    out_recv,
    part_send,
    part_recv,
    fwd_send,
    fwd_recv,
    pg_send,
    pg_recv,
    ng_send,
    ng_recv,
    loc_sem,
    hop,
    hop_g,
    cand,
    hop_send,
    hop_recv,
    cand_recv,
    src_send,
):
    c = lax.axis_index("ctx")
    h = lax.axis_index("head")
    toks = qb.shape[1]
    odd = lax.rem(c, 2) == 1
    even = lax.rem(c, 2) == 0
    mate = c + 1 - 2 * lax.rem(c, 2)
    side = lax.rem(c + 2 * lax.rem(c, 2) - 1 + n_ctx, n_ctx)
    has_side = jnp.logical_and(c > 0, c < n_ctx - 1)
    mid = n_ctx // 2
    subs = mid // N
    lane = lax.rem(c, mid)
    lane_piece = lax.div(lane, subs)
    is_low = c == mid - 1
    is_high = c == mid
    source = jnp.logical_or(is_low, c == mid - 2)
    near = c < mid - 2
    far = c > mid
    plain = jnp.logical_and(has_side, jnp.logical_not(jnp.logical_or(is_low, is_high)))
    gives = jnp.logical_and(jnp.logical_and(odd, c < n_ctx - 1), jnp.logical_not(is_low))
    takes = jnp.logical_and(even, c > 0)

    def cols(p):
        return pl.ds(pl.multiple_of(p * COLS, COLS), COLS)

    def piece(i):
        return lax.div(i, PIECES), pl.ds(pl.multiple_of(lax.rem(i, PIECES) * PIECE, PIECE), PIECE)

    def remote(src, dst, send, recv, place, head):
        return pltpu.make_async_remote_copy(
            src_ref=src, dst_ref=dst, send_sem=send, recv_sem=recv, device_id=(place, head), device_id_type=MESH
        )

    def mate_copy(i, src, dst, send, recv):
        a, rows = piece(i)
        return remote(src.at[a, rows], dst.at[a, rows], send.at[i], recv.at[i], mate, h)

    def side_copy(i, src, dst, send, recv):
        a, rows = piece(i)
        return remote(src.at[a, rows], dst.at[a, rows], send.at[i], recv.at[i], side, h)

    def part_of(i):
        a = lax.div(i, subs * PIECES)
        return a, pl.ds(pl.multiple_of(lax.rem(i, subs * PIECES) * (PIECE // subs), PIECE // subs), PIECE // subs)

    def send_parts():
        at = c - (mid - 2)

        def one(i, carry):
            a, rows = part_of(i)

            @pl.when(i < mid - 2)
            def _():
                remote(own.at[a, rows], hop.at[0, at], src_send.at[0], hop_recv.at[0], i, h).start()

            @pl.when(i >= mid - 2)
            def _():
                remote(own.at[a, rows], hop.at[1, at], src_send.at[0], hop_recv.at[1], mid + i, h).start()

            return carry

        lax.fori_loop(0, mid, one, 0)

    def give_grad(i):
        @pl.when(jnp.logical_and(takes, jnp.logical_not(is_high)))
        def _():
            side_copy(i, prev_g, next_in, ng_send, ng_recv).start()

        @pl.when(is_high)
        def _():
            for j in range(subs):
                to = i * subs + j
                a, rows = part_of(to)

                @pl.when(to > 0)
                def _():
                    remote(prev_g.at[a, rows], hop_g.at[0], ng_send.at[i], hop_recv.at[2], mid + to, h).start()

                @pl.when(to == 0)
                def _():
                    remote(prev_g.at[a, rows], hop_g.at[1], ng_send.at[i], hop_recv.at[3], 0, h).start()

    lane_a, lane_rows = part_of(lane)

    def arrived(k):
        ref = hop.at[k] if k < 2 else hop_g.at[k - 2]
        remote(ref, ref, hop_send.at[0], hop_recv.at[k], mid, h).wait_recv()

    def near_pair():
        return remote(hop.at[0], hop.at[1], hop_send.at[0], hop_recv.at[1], c + mid, h)

    def last_pair(k):
        return remote(hop.at[k], cand.at[:, lane_a, lane_rows], hop_send.at[k], cand_recv.at[lane_piece], mid, h)

    def far_grad():
        return remote(hop_g.at[0], hop_g.at[1], hop_send.at[2], hop_recv.at[3], c - mid, h)

    def last_grad(k, j):
        ref = next_in.at[lane_a, lane_rows]
        return remote(hop_g.at[k], ref, hop_send.at[3 + j], ng_recv.at[lane_piece], mid - 1 - j, h)

    def pass_far_grad():
        arrived(2)

        @pl.when(c < n_ctx - 1)
        def _():
            far_grad().start()

        @pl.when(c == n_ctx - 1)
        def _():
            for j in range(2):
                last_grad(0, j).start()

    def pass_near_grad():
        arrived(3)
        last_grad(1, 0).start()

        @pl.when(near)
        def _():
            last_grad(1, 1).start()

        @pl.when(c == mid - 2)
        def _():
            pltpu.make_async_copy(hop_g.at[1], next_in.at[lane_a, lane_rows], ng_recv.at[lane_piece]).start()

    def h_tok(r):
        return peer_of(h, r) * toks

    def in_copy(k, r):
        src, dst = ((q_ref, qb), (g_ref, gb))[k]
        p = peer_of(h, r)
        return remote(src.at[:, cols(p)], dst.at[r], in_send.at[k, r], in_recv.at[k, r], c, p)

    def out_copy(k, r):
        src, dst = ((ob, att_ref), (db, dq_ref))[k]
        p = peer_of(h, r)
        return remote(src.at[r], dst.at[:, cols(h)], out_send.at[k, r], out_recv.at[k, r], c, p)

    barrier = pltpu.get_barrier_semaphore()
    for r in range(1, 8):
        pl.semaphore_signal(barrier, inc=1, device_id=(c, peer_of(h, r)), device_id_type=MESH)
    pl.semaphore_signal(barrier, inc=1, device_id=(mate, h), device_id_type=MESH)

    own_copies = [pltpu.make_async_copy(ref, own.at[a], own_sem.at[a]) for a, ref in enumerate((k_ref, v_ref))]
    own_tiles = [
        pltpu.make_async_copy(ref.at[:, cols(h)], buf.at[0], own_sem.at[2 + a])
        for a, (ref, buf) in enumerate(((q_ref, qb), (g_ref, gb)))
    ]
    for copy in own_copies + own_tiles:
        copy.start()

    def greet(place):
        pl.semaphore_signal(barrier, inc=1, device_id=(place, h), device_id_type=MESH)

    @pl.when(plain)
    def _():
        greet(side)

    def greet_all(places):
        def one(i, carry):
            greet(places(i))
            return carry

        lax.fori_loop(0, mid, one, 0)

    @pl.when(source)
    def _():
        greet_all(lambda i: jnp.where(i < mid - 2, i, i + mid))

    @pl.when(is_high)
    def _():
        greet_all(lambda i: jnp.where(i > 0, i + mid, 0))

    @pl.when(near)
    def _():
        greet(mid - 2)
        greet(mid - 1)
        greet(c + mid)

    @pl.when(far)
    def _():
        greet(mid)

    @pl.when(jnp.logical_and(far, c < n_ctx - 2))
    def _():
        greet(c - mid)

    @pl.when(c >= n_ctx - 2)
    def _():
        greet(mid - 2)
        greet(mid - 1)

    def count(condition, number):
        return jnp.where(condition, number, 0)

    last_two = c >= n_ctx - 2
    pl.semaphore_wait(
        barrier,
        8
        + count(plain, 1)
        + count(jnp.logical_or(source, is_high), mid)
        + count(jnp.logical_or(near, last_two), 3)
        + count(jnp.logical_and(far, jnp.logical_not(last_two)), 2),
    )

    for copy in own_copies:
        copy.wait()

    @pl.when(source)
    def _():
        send_parts()

    def send_own(i, carry):
        mate_copy(i, own, part, part_send, part_recv).start()
        return carry

    lax.fori_loop(0, N, send_own, 0)

    def send_in(*tiles):
        for r in tiles:
            for k in range(2):
                in_copy(k, r).start()

    send_in(1, 7, 6)

    @pl.when(near)
    def _():
        arrived(0)

        @pl.when(c > 0)
        def _():
            near_pair().start()

        @pl.when(c == 0)
        def _():
            last_pair(0).start()

    send_in(3, 2)

    flip_all = jnp.full((PIECE, HD), owner_ref[c], jnp.int32) != c
    flip_low = jnp.full((PIECE, HD), owner_ref[mid - 1], jnp.int32) != mid - 1
    n_low = jnp.sum((img_ref[...] < c).astype(jnp.int32), axis=1, keepdims=True)

    def set_half(a, rows, upper, value):
        for b, (both, both_t) in enumerate(((kk, kkt), (vv, vvt))):

            @pl.when(a == b)
            def _():
                cut = slice(HD, None) if upper else slice(0, HD)
                both[rows, cut] = value.astype(BF16)
                both_t[cut, rows] = jnp.transpose(value).astype(BF16)

    def take(i, carry):
        a, rows = piece(i)
        mate_copy(i, own, part, part_send, part_recv).wait_recv()
        mine = own[a, rows].astype(F32)
        other = part[a, rows].astype(F32)
        upper = jnp.where(flip_all, other, mine)

        @pl.when(odd)
        def _():
            fwd[a, rows] = upper.astype(BF16)

            @pl.when(gives)
            def _():
                side_copy(i, fwd, low, fwd_send, fwd_recv).start()

            set_half(a, rows, False, jnp.where(flip_all, mine, other))

        set_half(a, rows, True, upper)

        @pl.when(i == LATE)
        def _():
            send_in(5, 4)

        @pl.when(jnp.logical_and(far, i == RELAY))
        def _():
            arrived(1)
            last_pair(1).start()

        return carry

    lax.fori_loop(0, N, take, 0)

    @pl.when(even)
    def _():
        @pl.when(jnp.logical_not(takes))
        def _():
            low[...] = jnp.zeros_like(low)

        def arrive(i, carry):
            a, rows = piece(i)

            @pl.when(jnp.logical_and(takes, jnp.logical_not(is_high)))
            def _():
                side_copy(i, fwd, low, fwd_send, fwd_recv).wait_recv()

            @pl.when(is_high)
            def _():
                both = cand.at[:, a, rows]
                remote(both, both, hop_send.at[0], cand_recv.at[i], mid, h).wait_recv()
                low[a, rows] = jnp.where(flip_low, cand[0, a, rows].astype(F32), cand[1, a, rows].astype(F32)).astype(BF16)

            set_half(a, rows, False, low[a, rows].astype(F32))
            return carry

        lax.fori_loop(0, N, arrive, 0)

    def step(i, carry):
        t = jnp.where(i == 0, 0, jnp.where(i == 1, 3, i - 1))
        r = 2 * t

        @pl.when(t == 0)
        def _():
            for copy in own_tiles:
                copy.wait()

        @pl.when(t > 0)
        def _():
            for k in range(2):
                in_copy(k, r).wait_recv()

        for k in range(2):
            in_copy(k, r + 1).wait_recv()

        @pl.when(i == 3)
        def _():
            for r_out in (7, 6, 3, 2):
                for k in range(2):
                    out_copy(k, r_out).start()

        att, dq = pair_step(
            (qb[r], qb[r + 1]),
            (gb[r], gb[r + 1]),
            (h_tok(r), h_tok(r + 1)),
            n_low,
            kk,
            vv,
            kkt,
            vvt,
            ps.at[t],
            dss.at[t],
            qs.at[t],
            gs.at[t],
        )
        for j in range(2):
            ob[r + j] = att[j]
            db[r + j] = dq[j]

        @pl.when(t == 0)
        def _():
            for a, (buf, ref) in enumerate(((ob, att_ref), (db, dq_ref))):
                pltpu.make_async_copy(buf.at[0], ref.at[:, cols(h)], loc_sem.at[a]).start()
            for k in range(2):
                out_copy(k, 1).start()

        @pl.when(i == 3)
        def _():
            for r_out in (5, 4):
                for k in range(2):
                    out_copy(k, r_out).start()

        return carry

    lax.fori_loop(0, 4, step, 0)

    for a, (left, right) in enumerate(((dss, qs), (ps, gs))):

        def sums(j, carry):
            i = a * PIECES + j
            rows = pl.ds(pl.multiple_of(j * PIECE, PIECE), PIECE)
            both = summed(left, right, rows)
            tot[...] = both * FACTOR if a == 0 else both

            @pl.when(even)
            def _():
                prev_g[a, rows] = tot[:, :HD].astype(BF16)
                give_grad(i)
                part_g[a, rows] = tot[:, HD:].astype(BF16)
                mate_copy(i, part_g, part_in, pg_send, pg_recv).start()
                fin[a, rows] = tot[:, HD:]

            @pl.when(odd)
            def _():
                @pl.when(gives)
                def _():
                    side_copy(i, prev_g, next_in, ng_send, ng_recv).wait_recv()
                    tot[:, HD:] += next_in[a, rows].astype(F32)

                lower = tot[:, :HD]
                upper = tot[:, HD:]
                part_g[a, rows] = jnp.where(flip_all, upper, lower).astype(BF16)
                mate_copy(i, part_g, part_in, pg_send, pg_recv).start()

                @pl.when(jnp.logical_and(far, i == FAR_GRAD))
                def _():
                    pass_far_grad()

                @pl.when(jnp.logical_and(near, i == NEAR_GRAD))
                def _():
                    pass_near_grad()

                mate_copy(i, part_g, part_in, pg_send, pg_recv).wait_recv()
                other = part_in[a, rows].astype(F32)
                fin[a, rows] = jnp.where(flip_all, lower + other, upper)

            return carry

        lax.fori_loop(0, PIECES, sums, 0)

    @pl.when(even)
    def _():
        @pl.when(far)
        def _():
            pass_far_grad()

        @pl.when(c < mid - 1)
        def _():
            pass_near_grad()

        def finish(i, carry):
            a, rows = piece(i)
            mate_copy(i, part_g, part_in, pg_send, pg_recv).wait_recv()
            other = part_in[a, rows].astype(F32)
            fin[a, rows] = jnp.where(flip_all, other, fin[a, rows] + other)
            return carry

        lax.fori_loop(0, N, finish, 0)

    @pl.when(source)
    def _():
        mine = flip_all == (jnp.full((PIECE, HD), c, jnp.int32) == mid - 2)

        def finish(i, carry):
            a, rows = piece(i)
            remote(next_in.at[a, rows], next_in.at[a, rows], hop_send.at[0], ng_recv.at[i], mid, h).wait_recv()
            other = next_in[a, rows].astype(F32)
            fin[a, rows] += jnp.where(mine, other, jnp.zeros_like(other))
            return carry

        lax.fori_loop(0, N, finish, 0)

    outs = [pltpu.make_async_copy(fin.at[a], ref, loc_sem.at[2 + a]) for a, ref in enumerate((dk_ref, dv_ref))]
    for copy in outs:
        copy.start()

    def drain(i, carry):
        for k in range(2):
            in_copy(k, i).wait_send()
            out_copy(k, i).wait()
        return carry

    lax.fori_loop(1, 8, drain, 0)

    def drain_pieces(i, carry):
        mate_copy(i, own, part, part_send, part_recv).wait_send()
        mate_copy(i, part_g, part_in, pg_send, pg_recv).wait_send()

        @pl.when(gives)
        def _():
            side_copy(i, fwd, low, fwd_send, fwd_recv).wait_send()

        @pl.when(takes)
        def _():
            side_copy(i, prev_g, next_in, ng_send, ng_recv).wait_send()

        return carry

    lax.fori_loop(0, N, drain_pieces, 0)

    @pl.when(source)
    def _():
        remote(own, part, src_send.at[0], hop_recv.at[0], mid, h).wait_send()

    @pl.when(near)
    def _():
        near_pair().wait_send()

    @pl.when(c < mid - 1)
    def _():
        last_grad(1, 0).wait_send()

    @pl.when(jnp.logical_or(near, c == n_ctx - 1))
    def _():
        last_grad(1, 1).wait_send()

    @pl.when(far)
    def _():
        last_pair(1).wait_send()

        @pl.when(c < n_ctx - 1)
        def _():
            far_grad().wait_send()

        @pl.when(c == n_ctx - 1)
        def _():
            last_grad(0, 0).wait_send()

    for a, (buf, ref) in enumerate(((ob, att_ref), (db, dq_ref))):
        pltpu.make_async_copy(buf.at[0], ref.at[:, cols(h)], loc_sem.at[a]).wait()
    for copy in outs:
        copy.wait()


def store(*refs):
    sources, targets, held, (in_sem, out_sem) = refs[:4], refs[4:8], refs[8:12], refs[12:]

    def copies(j, k):
        size = sources[j].shape[0] // CHUNKS
        rows = pl.ds(k * size, size)
        return (
            pltpu.make_async_copy(sources[j].at[rows], held[j].at[rows], in_sem.at[j, k]),
            pltpu.make_async_copy(held[j].at[rows], targets[j].at[rows], out_sem.at[j, k]),
        )

    every = [copies(j, k) for k in range(CHUNKS) for j in range(4)]
    for inward, _ in every:
        inward.start()
    for inward, outward in every:
        inward.wait()
        outward.start()
    for _, outward in every:
        outward.wait()


def per_device(n_ctx, query, d_out, keys_img, values_img, image_of, owner):
    toks = query.shape[0]
    anywhere = pl.BlockSpec(memory_space=pl.ANY)
    tile = pltpu.VMEM((8, toks, COLS), BF16)
    pair = pltpu.VMEM((2, ROWS, HD), BF16)
    part_rows = PIECE * N // (n_ctx // 2)
    dma = pltpu.SemaphoreType.DMA
    results = pl.pallas_call(
        functools.partial(kernel, n_ctx),
        out_shape=(
            jax.ShapeDtypeStruct(query.shape, BF16),
            jax.ShapeDtypeStruct(query.shape, BF16),
            jax.ShapeDtypeStruct(keys_img.shape, F32),
            jax.ShapeDtypeStruct(values_img.shape, F32),
        ),
        in_specs=[anywhere] * 4
        + [pl.BlockSpec(memory_space=pltpu.VMEM), pl.BlockSpec(memory_space=pltpu.SMEM)],
        out_specs=(anywhere,) * 4,
        scratch_shapes=[tile] * 4
        + [pair] * 4
        + [pltpu.VMEM((ROWS, 2 * HD), BF16)] * 2
        + [pltpu.VMEM((2 * HD, ROWS), BF16)] * 2
        + [pltpu.VMEM((4, ROWS, 2 * GROUP * toks), BF16)] * 2
        + [pltpu.VMEM((4, 2 * GROUP * toks, 2 * HD), BF16)] * 2
        + [pair] * 4
        + [pltpu.VMEM((2, ROWS, HD), F32)]
        + [pltpu.VMEM((PIECE, 2 * HD), F32)]
        + [dma((4,))]
        + [dma((2, 8))] * 4
        + [dma((N,))] * 8
        + [dma((4,))]
        + [pltpu.VMEM((2, 2, part_rows, HD), BF16), pltpu.VMEM((2, part_rows, HD), BF16), pltpu.VMEM((2, 2, ROWS, HD), BF16)]
        + [dma((5,)), dma((4,)), dma((N,)), dma((1,))],
        compiler_params=pltpu.CompilerParams(collective_id=0, has_side_effects=True, vmem_limit_bytes=60 << 20),
        name="attend",
    )(query, d_out, keys_img, values_img, image_of.reshape(1, -1), owner)
    return pl.pallas_call(
        store,
        out_shape=[jax.ShapeDtypeStruct(x.shape, x.dtype) for x in results],
        in_specs=[anywhere] * 4,
        out_specs=[anywhere] * 4,
        scratch_shapes=[pltpu.VMEM(x.shape, x.dtype) for x in results] + [dma((4, CHUNKS))] * 2,
        name="store",
    )(*results)


def solution(mesh):
    placed = (
        P(("ctx", "head"), None),
        P(("ctx", "head"), None),
        P("ctx", "head"),
        P("ctx", "head"),
        P("ctx"),
        P(),
    )
    return jax.shard_map(
        functools.partial(per_device, mesh.shape["ctx"]),
        mesh=mesh,
        in_specs=placed,
        out_specs=(
            P(("ctx", "head"), None),
            P(("ctx", "head"), None),
            P("ctx", "head"),
            P("ctx", "head"),
        ),
        check_vma=False,
    )
```

```python
import functools

import jax
import jax.numpy as jnp
from jax import lax
from jax.experimental import pallas as pl
from jax.experimental.pallas import tpu as pltpu
from jax.sharding import PartitionSpec as P

HD = 128
GROUP = 8
COLS = GROUP * HD
ROWS = 1024
PIECE = 256
PIECES = ROWS // PIECE
N = 2 * PIECES
FACTOR = HD**-0.5
LOG2E = 1.4426950408889634
CHUNKS = 2
LATE = 5
FAR_GRAD, NEAR_GRAD = 3, 7
MESH = pl.DeviceIdType.MESH
BF16 = jnp.bfloat16
F32 = jnp.float32


def peer_of(h, r):
    b0 = lax.rem(h + r, 2)
    b1 = lax.rem(lax.div(h, 2) + lax.div(r, 2), 2)
    b2 = lax.rem(lax.div(h, 4) + lax.div(r, 4), 2)
    return b0 + 2 * b1 + 4 * b2


def stacked(tile):
    return jnp.concatenate([tile[:, j * HD : (j + 1) * HD] for j in range(GROUP)], axis=0)


def unstacked(rows, toks):
    return jnp.concatenate([rows[j * toks : (j + 1) * toks] for j in range(GROUP)], axis=1)


def pair_step(q_tiles, g_tiles, firsts, n_low, kk, vv, kkt, vvt, p_ref, ds_ref, qs_ref, gs_ref):
    toks = q_tiles[0].shape[0]
    each = toks * GROUP
    rows = 2 * each
    q2 = jnp.concatenate([stacked(tile) for tile in q_tiles], axis=0).astype(F32)
    g2 = jnp.concatenate([stacked(tile) for tile in g_tiles], axis=0).astype(F32)

    def is_low(shape, axis):
        at = lax.broadcasted_iota(jnp.int32, shape, axis)
        return lax.rem(at, toks) + jnp.where(at < each, firsts[0], firsts[1]) < n_low

    low_lane = is_low((HD, rows), 1)
    low_row = is_low((rows, HD), 0)

    def halves(x, mask, axis):
        zero = jnp.zeros_like(x)
        return jnp.concatenate([jnp.where(mask, x, zero), jnp.where(mask, zero, x)], axis=axis).astype(BF16)

    qt = jnp.transpose(q2)
    gt = jnp.transpose(g2)
    st = jnp.dot(kk[...], halves(qt, low_lane, 0), preferred_element_type=F32)
    top = jnp.max(st, axis=0, keepdims=True)
    ex = jnp.exp2((st - top) * (FACTOR * LOG2E))
    inv = 1.0 / jnp.sum(ex, axis=0, keepdims=True)
    p = ex.astype(BF16)
    p_ref[...] = p
    inv_row = jnp.transpose(jnp.broadcast_to(inv, (HD, rows)))
    qs_ref[...] = halves(q2 * inv_row, low_row, 1)
    gs_ref[...] = halves(g2 * inv_row, low_row, 1)
    ot = jnp.dot(vvt[...], p, preferred_element_type=F32)
    ot = (jnp.where(low_lane, ot[:HD], ot[HD:]) * inv).astype(BF16).astype(F32)
    delta = jnp.sum(gt * ot, axis=0, keepdims=True)
    dp = jnp.dot(vv[...], halves(gt, low_lane, 0), preferred_element_type=F32)
    ds = (p.astype(F32) * (dp - delta)).astype(BF16)
    ds_ref[...] = ds
    dqt = jnp.dot(kkt[...], ds, preferred_element_type=F32)
    dqt = jnp.where(low_lane, dqt[:HD], dqt[HD:]) * (inv * FACTOR)
    att = jnp.transpose(ot).astype(BF16)
    dq = jnp.transpose(dqt).astype(BF16)
    return (
        [unstacked(att[:each], toks), unstacked(att[each:], toks)],
        [unstacked(dq[:each], toks), unstacked(dq[each:], toks)],
    )


def summed(left, right, rows):
    total = jnp.dot(left[0, rows], right[0], preferred_element_type=F32)
    for t in range(1, left.shape[0]):
        total = total + jnp.dot(left[t, rows], right[t], preferred_element_type=F32)
    return total


def kernel(
    n_ctx,
    q_ref,
    g_ref,
    k_ref,
    v_ref,
    img_ref,
    owner_ref,
    att_ref,
    dq_ref,
    dk_ref,
    dv_ref,
    qb,
    gb,
    ob,
    db,
    own,
    part,
    low,
    fwd,
    kk,
    vv,
    kkt,
    vvt,
    ps,
    dss,
    qs,
    gs,
    part_g,
    prev_g,
    part_in,
    next_in,
    fin,
    tot,
    own_sem,
    in_send,
    in_recv,
    out_send,
    out_recv,
    part_send,
    part_recv,
    fwd_send,
    fwd_recv,
    pg_send,
    pg_recv,
    ng_send,
    ng_recv,
    loc_sem,
    hop,
    chosen,
    hop_g,
    hop_send,
    hop_recv,
    cand_recv,
    src_send,
):
    c = lax.axis_index("ctx")
    h = lax.axis_index("head")
    toks = qb.shape[1]
    odd = lax.rem(c, 2) == 1
    even = lax.rem(c, 2) == 0
    mate = c + 1 - 2 * lax.rem(c, 2)
    side = lax.rem(c + 2 * lax.rem(c, 2) - 1 + n_ctx, n_ctx)
    has_side = jnp.logical_and(c > 0, c < n_ctx - 1)
    mid = n_ctx // 2
    subs = mid // N
    lane = lax.rem(c, mid)
    lane_piece = lax.div(lane, subs)
    is_low = c == mid - 1
    is_high = c == mid
    source = jnp.logical_or(is_low, c == mid - 2)
    near = c < mid - 2
    far = c > mid
    plain = jnp.logical_and(has_side, jnp.logical_not(jnp.logical_or(is_low, is_high)))
    gives = jnp.logical_and(jnp.logical_and(odd, c < n_ctx - 1), jnp.logical_not(is_low))
    takes = jnp.logical_and(even, c > 0)

    def cols(p):
        return pl.ds(pl.multiple_of(p * COLS, COLS), COLS)

    def piece(i):
        return lax.div(i, PIECES), pl.ds(pl.multiple_of(lax.rem(i, PIECES) * PIECE, PIECE), PIECE)

    def remote(src, dst, send, recv, place, head):
        return pltpu.make_async_remote_copy(
            src_ref=src, dst_ref=dst, send_sem=send, recv_sem=recv, device_id=(place, head), device_id_type=MESH
        )

    def mate_copy(i, src, dst, send, recv):
        a, rows = piece(i)
        return remote(src.at[a, rows], dst.at[a, rows], send.at[i], recv.at[i], mate, h)

    def side_copy(i, src, dst, send, recv):
        a, rows = piece(i)
        return remote(src.at[a, rows], dst.at[a, rows], send.at[i], recv.at[i], side, h)

    def part_of(i):
        a = lax.div(i, subs * PIECES)
        return a, pl.ds(pl.multiple_of(lax.rem(i, subs * PIECES) * (PIECE // subs), PIECE // subs), PIECE // subs)

    def send_parts():
        at = c - (mid - 2)

        def one(i, carry):
            a, rows = part_of(i)

            @pl.when(i < mid - 2)
            def _():
                remote(own.at[a, rows], hop.at[at], src_send.at[0], hop_recv.at[0], i, h).start()

            @pl.when(i >= mid - 2)
            def _():
                remote(own.at[a, rows], hop.at[at], src_send.at[0], hop_recv.at[0], mid + i, h).start()

            return carry

        lax.fori_loop(0, mid, one, 0)

    def give_grad(i):
        @pl.when(jnp.logical_and(takes, jnp.logical_not(is_high)))
        def _():
            side_copy(i, prev_g, next_in, ng_send, ng_recv).start()

        @pl.when(is_high)
        def _():
            for j in range(subs):
                to = i * subs + j
                a, rows = part_of(to)

                @pl.when(to > 0)
                def _():
                    remote(prev_g.at[a, rows], hop_g.at[0], ng_send.at[i], hop_recv.at[2], mid + to, h).start()

                @pl.when(to == 0)
                def _():
                    remote(prev_g.at[a, rows], hop_g.at[1], ng_send.at[i], hop_recv.at[3], 0, h).start()

    lane_a, lane_rows = part_of(lane)

    def arrived(k):
        ref = hop if k == 0 else chosen if k == 1 else hop_g.at[k - 2]
        remote(ref, ref, hop_send.at[0], hop_recv.at[k], mid, h).wait_recv()

    def choose():
        flipped = jnp.full(chosen.shape, owner_ref[mid - 1], jnp.int32) != mid - 1
        chosen[...] = jnp.where(flipped, hop[0].astype(F32), hop[1].astype(F32)).astype(BF16)

    def near_pair():
        return remote(chosen, chosen, hop_send.at[0], hop_recv.at[1], c + mid, h)

    def last_pair():
        return remote(chosen, low.at[lane_a, lane_rows], hop_send.at[1], cand_recv.at[lane_piece], mid, h)

    def pass_near():
        arrived(0)
        choose()

        @pl.when(c > 0)
        def _():
            near_pair().start()

        @pl.when(c == 0)
        def _():
            last_pair().start()

    def pass_far():
        @pl.when(c < n_ctx - 2)
        def _():
            arrived(1)

        @pl.when(c >= n_ctx - 2)
        def _():
            arrived(0)
            choose()

        last_pair().start()

    def far_grad():
        return remote(hop_g.at[0], hop_g.at[1], hop_send.at[2], hop_recv.at[3], c - mid, h)

    def last_grad(k, j):
        ref = next_in.at[lane_a, lane_rows]
        return remote(hop_g.at[k], ref, hop_send.at[3 + j], ng_recv.at[lane_piece], mid - 1 - j, h)

    def pass_far_grad():
        arrived(2)

        @pl.when(c < n_ctx - 1)
        def _():
            far_grad().start()

        @pl.when(c == n_ctx - 1)
        def _():
            for j in range(2):
                last_grad(0, j).start()

    def pass_near_grad():
        arrived(3)
        last_grad(1, 0).start()

        @pl.when(near)
        def _():
            last_grad(1, 1).start()

        @pl.when(c == mid - 2)
        def _():
            pltpu.make_async_copy(hop_g.at[1], next_in.at[lane_a, lane_rows], ng_recv.at[lane_piece]).start()

    def h_tok(r):
        return peer_of(h, r) * toks

    def in_copy(k, r):
        src, dst = ((q_ref, qb), (g_ref, gb))[k]
        p = peer_of(h, r)
        return remote(src.at[:, cols(p)], dst.at[r], in_send.at[k, r], in_recv.at[k, r], c, p)

    def out_copy(k, r):
        src, dst = ((ob, att_ref), (db, dq_ref))[k]
        p = peer_of(h, r)
        return remote(src.at[r], dst.at[:, cols(h)], out_send.at[k, r], out_recv.at[k, r], c, p)

    barrier = pltpu.get_barrier_semaphore()
    for r in range(1, 8):
        pl.semaphore_signal(barrier, inc=1, device_id=(c, peer_of(h, r)), device_id_type=MESH)
    pl.semaphore_signal(barrier, inc=1, device_id=(mate, h), device_id_type=MESH)

    own_copies = [pltpu.make_async_copy(ref, own.at[a], own_sem.at[a]) for a, ref in enumerate((k_ref, v_ref))]
    own_tiles = [
        pltpu.make_async_copy(ref.at[:, cols(h)], buf.at[0], own_sem.at[2 + a])
        for a, (ref, buf) in enumerate(((q_ref, qb), (g_ref, gb)))
    ]
    for copy in own_copies + own_tiles:
        copy.start()

    def greet(place):
        pl.semaphore_signal(barrier, inc=1, device_id=(place, h), device_id_type=MESH)

    @pl.when(plain)
    def _():
        greet(side)

    def greet_all(places):
        def one(i, carry):
            greet(places(i))
            return carry

        lax.fori_loop(0, mid, one, 0)

    @pl.when(is_high)
    def _():
        greet_all(lambda i: jnp.where(i > 0, i + mid, 0))

    @pl.when(jnp.logical_or(near, c >= n_ctx - 2))
    def _():
        greet(mid - 2)
        greet(mid - 1)

    @pl.when(jnp.logical_and(far, c < n_ctx - 2))
    def _():
        greet(c - mid)

    def count(condition, number):
        return jnp.where(condition, number, 0)

    pl.semaphore_wait(
        barrier, 8 + count(plain, 1) + count(source, mid) + count(jnp.logical_or(near, far), 1)
    )

    for copy in own_copies:
        copy.wait()

    @pl.when(source)
    def _():
        send_parts()

    def send_own(i, carry):
        mate_copy(i, own, part, part_send, part_recv).start()
        return carry

    lax.fori_loop(0, N, send_own, 0)

    def send_in(*tiles):
        for r in tiles:
            for k in range(2):
                in_copy(k, r).start()

    send_in(1, 7, 6, 3, 2)

    flip_all = jnp.full((PIECE, HD), owner_ref[c], jnp.int32) != c
    n_low = jnp.sum((img_ref[...] < c).astype(jnp.int32), axis=1, keepdims=True)

    def set_half(a, rows, upper, value):
        for b, (both, both_t) in enumerate(((kk, kkt), (vv, vvt))):

            @pl.when(a == b)
            def _():
                cut = slice(HD, None) if upper else slice(0, HD)
                both[rows, cut] = value.astype(BF16)
                both_t[cut, rows] = jnp.transpose(value).astype(BF16)

    near_turn = jnp.maximum(N - 2 - lane_piece, 0)
    far_turn = jnp.minimum(N - 1 - lax.div(lane_piece - 3 + 8, 2) + 4, N - 1)

    def take(i, carry):
        a, rows = piece(i)
        mate_copy(i, own, part, part_send, part_recv).wait_recv()
        mine = own[a, rows].astype(F32)
        other = part[a, rows].astype(F32)
        upper = jnp.where(flip_all, other, mine)

        @pl.when(odd)
        def _():
            fwd[a, rows] = upper.astype(BF16)

            @pl.when(gives)
            def _():
                side_copy(i, fwd, low, fwd_send, fwd_recv).start()

            set_half(a, rows, False, jnp.where(flip_all, mine, other))

        set_half(a, rows, True, upper)

        @pl.when(i == LATE)
        def _():
            send_in(5, 4)

        @pl.when(jnp.logical_and(near, i == near_turn))
        def _():
            pass_near()

        @pl.when(jnp.logical_and(far, i == far_turn))
        def _():
            pass_far()

        return carry

    lax.fori_loop(0, N, take, 0)

    @pl.when(even)
    def _():
        @pl.when(jnp.logical_not(takes))
        def _():
            low[...] = jnp.zeros_like(low)

        def arrive(i, carry):
            a, rows = piece(i)

            @pl.when(jnp.logical_and(takes, jnp.logical_not(is_high)))
            def _():
                side_copy(i, fwd, low, fwd_send, fwd_recv).wait_recv()

            @pl.when(is_high)
            def _():
                remote(low.at[a, rows], low.at[a, rows], hop_send.at[0], cand_recv.at[i], mid, h).wait_recv()

            set_half(a, rows, False, low[a, rows].astype(F32))
            return carry

        lax.fori_loop(0, N, arrive, 0)

    def step(i, carry):
        t = jnp.where(i == 0, 0, jnp.where(i == 1, 3, i - 1))
        r = 2 * t

        @pl.when(t == 0)
        def _():
            for copy in own_tiles:
                copy.wait()

        @pl.when(t > 0)
        def _():
            for k in range(2):
                in_copy(k, r).wait_recv()

        for k in range(2):
            in_copy(k, r + 1).wait_recv()

        @pl.when(jnp.logical_and(i == 3, jnp.logical_not(is_high)))
        def _():
            for r_out in (7, 6, 3, 2):
                for k in range(2):
                    out_copy(k, r_out).start()

        att, dq = pair_step(
            (qb[r], qb[r + 1]),
            (gb[r], gb[r + 1]),
            (h_tok(r), h_tok(r + 1)),
            n_low,
            kk,
            vv,
            kkt,
            vvt,
            ps.at[t],
            dss.at[t],
            qs.at[t],
            gs.at[t],
        )
        for j in range(2):
            ob[r + j] = att[j]
            db[r + j] = dq[j]

        @pl.when(t == 0)
        def _():
            for a, (buf, ref) in enumerate(((ob, att_ref), (db, dq_ref))):
                pltpu.make_async_copy(buf.at[0], ref.at[:, cols(h)], loc_sem.at[a]).start()
            for k in range(2):
                out_copy(k, 1).start()

        @pl.when(jnp.logical_or(i == 3, jnp.logical_and(is_high, i > 0)))
        def _():
            for j in (1, 0):
                for k in range(2):
                    out_copy(k, r + j).start()

        return carry

    lax.fori_loop(0, 4, step, 0)

    for a, (left, right) in enumerate(((dss, qs), (ps, gs))):

        def sums(j, carry):
            i = a * PIECES + j
            rows = pl.ds(pl.multiple_of(j * PIECE, PIECE), PIECE)
            both = summed(left, right, rows)
            tot[...] = both * FACTOR if a == 0 else both

            @pl.when(even)
            def _():
                prev_g[a, rows] = tot[:, :HD].astype(BF16)
                give_grad(i)
                part_g[a, rows] = tot[:, HD:].astype(BF16)
                mate_copy(i, part_g, part_in, pg_send, pg_recv).start()
                fin[a, rows] = tot[:, HD:]

            @pl.when(odd)
            def _():
                @pl.when(gives)
                def _():
                    side_copy(i, prev_g, next_in, ng_send, ng_recv).wait_recv()
                    tot[:, HD:] += next_in[a, rows].astype(F32)

                lower = tot[:, :HD]
                upper = tot[:, HD:]
                part_g[a, rows] = jnp.where(flip_all, upper, lower).astype(BF16)
                mate_copy(i, part_g, part_in, pg_send, pg_recv).start()

                @pl.when(jnp.logical_and(far, i == FAR_GRAD))
                def _():
                    pass_far_grad()

                @pl.when(jnp.logical_and(near, i == NEAR_GRAD))
                def _():
                    pass_near_grad()

                mate_copy(i, part_g, part_in, pg_send, pg_recv).wait_recv()
                other = part_in[a, rows].astype(F32)
                fin[a, rows] = jnp.where(flip_all, lower + other, upper)

            return carry

        lax.fori_loop(0, PIECES, sums, 0)

    @pl.when(even)
    def _():
        @pl.when(far)
        def _():
            pass_far_grad()

        @pl.when(c < mid - 1)
        def _():
            pass_near_grad()

        def finish(i, carry):
            a, rows = piece(i)
            mate_copy(i, part_g, part_in, pg_send, pg_recv).wait_recv()
            other = part_in[a, rows].astype(F32)
            fin[a, rows] = jnp.where(flip_all, other, fin[a, rows] + other)
            return carry

        lax.fori_loop(0, N, finish, 0)

    @pl.when(source)
    def _():
        mine = flip_all == (jnp.full((PIECE, HD), c, jnp.int32) == mid - 2)

        def finish(i, carry):
            a, rows = piece(i)
            remote(next_in.at[a, rows], next_in.at[a, rows], hop_send.at[0], ng_recv.at[i], mid, h).wait_recv()
            other = next_in[a, rows].astype(F32)
            fin[a, rows] += jnp.where(mine, other, jnp.zeros_like(other))
            return carry

        lax.fori_loop(0, N, finish, 0)

    outs = [pltpu.make_async_copy(fin.at[a], ref, loc_sem.at[2 + a]) for a, ref in enumerate((dk_ref, dv_ref))]
    for copy in outs:
        copy.start()

    def drain(i, carry):
        for k in range(2):
            in_copy(k, i).wait_send()
            out_copy(k, i).wait()
        return carry

    lax.fori_loop(1, 8, drain, 0)

    def drain_pieces(i, carry):
        mate_copy(i, own, part, part_send, part_recv).wait_send()
        mate_copy(i, part_g, part_in, pg_send, pg_recv).wait_send()

        @pl.when(gives)
        def _():
            side_copy(i, fwd, low, fwd_send, fwd_recv).wait_send()

        @pl.when(takes)
        def _():
            side_copy(i, prev_g, next_in, ng_send, ng_recv).wait_send()

        return carry

    lax.fori_loop(0, N, drain_pieces, 0)

    @pl.when(source)
    def _():
        remote(own, part, src_send.at[0], hop_recv.at[0], mid, h).wait_send()

    @pl.when(jnp.logical_and(near, c > 0))
    def _():
        near_pair().wait_send()

    @pl.when(jnp.logical_or(c == 0, far))
    def _():
        last_pair().wait_send()

    @pl.when(c < mid - 1)
    def _():
        last_grad(1, 0).wait_send()

    @pl.when(jnp.logical_or(near, c == n_ctx - 1))
    def _():
        last_grad(1, 1).wait_send()

    @pl.when(far)
    def _():
        @pl.when(c < n_ctx - 1)
        def _():
            far_grad().wait_send()

        @pl.when(c == n_ctx - 1)
        def _():
            last_grad(0, 0).wait_send()

    for a, (buf, ref) in enumerate(((ob, att_ref), (db, dq_ref))):
        pltpu.make_async_copy(buf.at[0], ref.at[:, cols(h)], loc_sem.at[a]).wait()
    for copy in outs:
        copy.wait()


def store(*refs):
    sources, targets, held, (in_sem, out_sem) = refs[:4], refs[4:8], refs[8:12], refs[12:]

    def copies(j, k):
        size = sources[j].shape[0] // CHUNKS
        rows = pl.ds(k * size, size)
        return (
            pltpu.make_async_copy(sources[j].at[rows], held[j].at[rows], in_sem.at[j, k]),
            pltpu.make_async_copy(held[j].at[rows], targets[j].at[rows], out_sem.at[j, k]),
        )

    every = [copies(j, k) for k in range(CHUNKS) for j in range(4)]
    for inward, _ in every:
        inward.start()
    for inward, outward in every:
        inward.wait()
        outward.start()
    for _, outward in every:
        outward.wait()


def per_device(n_ctx, query, d_out, keys_img, values_img, image_of, owner):
    toks = query.shape[0]
    anywhere = pl.BlockSpec(memory_space=pl.ANY)
    tile = pltpu.VMEM((8, toks, COLS), BF16)
    pair = pltpu.VMEM((2, ROWS, HD), BF16)
    part_rows = PIECE * N // (n_ctx // 2)
    dma = pltpu.SemaphoreType.DMA
    results = pl.pallas_call(
        functools.partial(kernel, n_ctx),
        out_shape=(
            jax.ShapeDtypeStruct(query.shape, BF16),
            jax.ShapeDtypeStruct(query.shape, BF16),
            jax.ShapeDtypeStruct(keys_img.shape, F32),
            jax.ShapeDtypeStruct(values_img.shape, F32),
        ),
        in_specs=[anywhere] * 4
        + [pl.BlockSpec(memory_space=pltpu.VMEM), pl.BlockSpec(memory_space=pltpu.SMEM)],
        out_specs=(anywhere,) * 4,
        scratch_shapes=[tile] * 4
        + [pair] * 4
        + [pltpu.VMEM((ROWS, 2 * HD), BF16)] * 2
        + [pltpu.VMEM((2 * HD, ROWS), BF16)] * 2
        + [pltpu.VMEM((4, ROWS, 2 * GROUP * toks), BF16)] * 2
        + [pltpu.VMEM((4, 2 * GROUP * toks, 2 * HD), BF16)] * 2
        + [pair] * 4
        + [pltpu.VMEM((2, ROWS, HD), F32)]
        + [pltpu.VMEM((PIECE, 2 * HD), F32)]
        + [dma((4,))]
        + [dma((2, 8))] * 4
        + [dma((N,))] * 8
        + [dma((4,))]
        + [pltpu.VMEM((2, part_rows, HD), BF16), pltpu.VMEM((part_rows, HD), BF16), pltpu.VMEM((2, part_rows, HD), BF16)]
        + [dma((5,)), dma((4,)), dma((N,)), dma((1,))],
        compiler_params=pltpu.CompilerParams(collective_id=0, has_side_effects=True, vmem_limit_bytes=60 << 20),
        name="attend",
    )(query, d_out, keys_img, values_img, image_of.reshape(1, -1), owner)
    return pl.pallas_call(
        store,
        out_shape=[jax.ShapeDtypeStruct(x.shape, x.dtype) for x in results],
        in_specs=[anywhere] * 4,
        out_specs=[anywhere] * 4,
        scratch_shapes=[pltpu.VMEM(x.shape, x.dtype) for x in results] + [dma((4, CHUNKS))] * 2,
        name="store",
    )(*results)


def solution(mesh):
    placed = (
        P(("ctx", "head"), None),
        P(("ctx", "head"), None),
        P("ctx", "head"),
        P("ctx", "head"),
        P("ctx"),
        P(),
    )
    return jax.shard_map(
        functools.partial(per_device, mesh.shape["ctx"]),
        mesh=mesh,
        in_specs=placed,
        out_specs=(
            P(("ctx", "head"), None),
            P(("ctx", "head"), None),
            P("ctx", "head"),
            P("ctx", "head"),
        ),
        check_vma=False,
    )
```

```python
import functools

import jax
import jax.numpy as jnp
from jax import lax
from jax.experimental import pallas as pl
from jax.experimental.pallas import tpu as pltpu
from jax.sharding import PartitionSpec as P

HD = 128
GROUP = 8
COLS = GROUP * HD
ROWS = 1024
PIECE = 256
PIECES = ROWS // PIECE
N = 2 * PIECES
FACTOR = HD**-0.5
LOG2E = 1.4426950408889634
CHUNKS = 2
LATE = 5
FAR_GRAD, NEAR_GRAD = 3, 7
MESH = pl.DeviceIdType.MESH
BF16 = jnp.bfloat16
F32 = jnp.float32


def peer_of(h, r):
    b0 = lax.rem(h + r, 2)
    b1 = lax.rem(lax.div(h, 2) + lax.div(r, 2), 2)
    b2 = lax.rem(lax.div(h, 4) + lax.div(r, 4), 2)
    return b0 + 2 * b1 + 4 * b2


def stacked(tile):
    return jnp.concatenate([tile[:, j * HD : (j + 1) * HD] for j in range(GROUP)], axis=0)


def unstacked(rows, toks):
    return jnp.concatenate([rows[j * toks : (j + 1) * toks] for j in range(GROUP)], axis=1)


def pair_step(q_tiles, g_tiles, firsts, n_low, kk, vv, kkt, vvt, p_ref, ds_ref, qs_ref, gs_ref):
    toks = q_tiles[0].shape[0]
    each = toks * GROUP
    rows = 2 * each
    q2 = jnp.concatenate([stacked(tile) for tile in q_tiles], axis=0).astype(F32)
    g2 = jnp.concatenate([stacked(tile) for tile in g_tiles], axis=0).astype(F32)

    def is_low(shape, axis):
        at = lax.broadcasted_iota(jnp.int32, shape, axis)
        return lax.rem(at, toks) + jnp.where(at < each, firsts[0], firsts[1]) < n_low

    low_lane = is_low((HD, rows), 1)
    low_row = is_low((rows, HD), 0)

    def halves(x, mask, axis):
        zero = jnp.zeros_like(x)
        return jnp.concatenate([jnp.where(mask, x, zero), jnp.where(mask, zero, x)], axis=axis).astype(BF16)

    qt = jnp.transpose(q2)
    gt = jnp.transpose(g2)
    st = jnp.dot(kk[...], halves(qt, low_lane, 0), preferred_element_type=F32)
    top = jnp.max(st, axis=0, keepdims=True)
    ex = jnp.exp2((st - top) * (FACTOR * LOG2E))
    inv = 1.0 / jnp.sum(ex, axis=0, keepdims=True)
    p = ex.astype(BF16)
    p_ref[...] = p
    inv_row = jnp.transpose(jnp.broadcast_to(inv, (HD, rows)))
    qs_ref[...] = halves(q2 * inv_row, low_row, 1)
    gs_ref[...] = halves(g2 * inv_row, low_row, 1)
    ot = jnp.dot(vvt[...], p, preferred_element_type=F32)
    ot = (jnp.where(low_lane, ot[:HD], ot[HD:]) * inv).astype(BF16).astype(F32)
    delta = jnp.sum(gt * ot, axis=0, keepdims=True)
    dp = jnp.dot(vv[...], halves(gt, low_lane, 0), preferred_element_type=F32)
    ds = (p.astype(F32) * (dp - delta)).astype(BF16)
    ds_ref[...] = ds
    dqt = jnp.dot(kkt[...], ds, preferred_element_type=F32)
    dqt = jnp.where(low_lane, dqt[:HD], dqt[HD:]) * (inv * FACTOR)
    att = jnp.transpose(ot).astype(BF16)
    dq = jnp.transpose(dqt).astype(BF16)
    return (
        [unstacked(att[:each], toks), unstacked(att[each:], toks)],
        [unstacked(dq[:each], toks), unstacked(dq[each:], toks)],
    )


def summed(left, right, rows):
    total = jnp.dot(left[0, rows], right[0], preferred_element_type=F32)
    for t in range(1, left.shape[0]):
        total = total + jnp.dot(left[t, rows], right[t], preferred_element_type=F32)
    return total


def kernel(
    n_ctx,
    q_ref,
    g_ref,
    k_ref,
    v_ref,
    img_ref,
    owner_ref,
    att_ref,
    dq_ref,
    dk_ref,
    dv_ref,
    qb,
    gb,
    ob,
    db,
    own,
    part,
    low,
    fwd,
    kk,
    vv,
    kkt,
    vvt,
    ps,
    dss,
    qs,
    gs,
    part_g,
    prev_g,
    part_in,
    next_in,
    fin,
    tot,
    own_sem,
    in_send,
    in_recv,
    out_send,
    out_recv,
    part_send,
    part_recv,
    fwd_send,
    fwd_recv,
    pg_send,
    pg_recv,
    ng_send,
    ng_recv,
    loc_sem,
    hop,
    chosen,
    hop_g,
    hop_send,
    hop_recv,
    cand_recv,
    src_send,
):
    c = lax.axis_index("ctx")
    h = lax.axis_index("head")
    toks = qb.shape[1]
    odd = lax.rem(c, 2) == 1
    even = lax.rem(c, 2) == 0
    mate = c + 1 - 2 * lax.rem(c, 2)
    side = lax.rem(c + 2 * lax.rem(c, 2) - 1 + n_ctx, n_ctx)
    has_side = jnp.logical_and(c > 0, c < n_ctx - 1)
    mid = n_ctx // 2
    subs = mid // N
    lane = lax.rem(c, mid)
    lane_piece = lax.div(lane, subs)
    is_low = c == mid - 1
    is_high = c == mid
    source = jnp.logical_or(is_low, c == mid - 2)
    near = c < mid - 2
    far = c > mid
    plain = jnp.logical_and(has_side, jnp.logical_not(jnp.logical_or(is_low, is_high)))
    gives = jnp.logical_and(jnp.logical_and(odd, c < n_ctx - 1), jnp.logical_not(is_low))
    takes = jnp.logical_and(even, c > 0)

    def cols(p):
        return pl.ds(pl.multiple_of(p * COLS, COLS), COLS)

    def piece(i):
        return lax.div(i, PIECES), pl.ds(pl.multiple_of(lax.rem(i, PIECES) * PIECE, PIECE), PIECE)

    def remote(src, dst, send, recv, place, head):
        return pltpu.make_async_remote_copy(
            src_ref=src, dst_ref=dst, send_sem=send, recv_sem=recv, device_id=(place, head), device_id_type=MESH
        )

    def mate_copy(i, src, dst, send, recv):
        a, rows = piece(i)
        return remote(src.at[a, rows], dst.at[a, rows], send.at[i], recv.at[i], mate, h)

    def side_copy(i, src, dst, send, recv):
        a, rows = piece(i)
        return remote(src.at[a, rows], dst.at[a, rows], send.at[i], recv.at[i], side, h)

    def part_of(i):
        a = lax.div(i, subs * PIECES)
        return a, pl.ds(pl.multiple_of(lax.rem(i, subs * PIECES) * (PIECE // subs), PIECE // subs), PIECE // subs)

    def send_parts():
        at = c - (mid - 2)

        def one(i, carry):
            a, rows = part_of(i)

            @pl.when(i < mid - 2)
            def _():
                remote(own.at[a, rows], hop.at[at], src_send.at[0], hop_recv.at[0], i, h).start()

            @pl.when(i >= mid - 2)
            def _():
                remote(own.at[a, rows], hop.at[at], src_send.at[0], hop_recv.at[0], mid + i, h).start()

            return carry

        lax.fori_loop(0, mid, one, 0)

    def give_grad(i):
        @pl.when(jnp.logical_and(takes, jnp.logical_not(is_high)))
        def _():
            side_copy(i, prev_g, next_in, ng_send, ng_recv).start()

        @pl.when(is_high)
        def _():
            for j in range(subs):
                to = i * subs + j
                a, rows = part_of(to)

                @pl.when(to > 0)
                def _():
                    remote(prev_g.at[a, rows], hop_g.at[0], ng_send.at[i], hop_recv.at[2], mid + to, h).start()

                @pl.when(to == 0)
                def _():
                    remote(prev_g.at[a, rows], hop_g.at[1], ng_send.at[i], hop_recv.at[3], 0, h).start()

    lane_a, lane_rows = part_of(lane)

    def arrived(k):
        ref = hop if k == 0 else chosen if k == 1 else hop_g.at[k - 2]
        remote(ref, ref, hop_send.at[0], hop_recv.at[k], mid, h).wait_recv()

    def choose():
        flipped = jnp.full(chosen.shape, owner_ref[mid - 1], jnp.int32) != mid - 1
        chosen[...] = jnp.where(flipped, hop[0].astype(F32), hop[1].astype(F32)).astype(BF16)

    def near_pair():
        return remote(chosen, chosen, hop_send.at[0], hop_recv.at[1], c + mid, h)

    def last_pair():
        return remote(chosen, low.at[lane_a, lane_rows], hop_send.at[1], cand_recv.at[lane_piece], mid, h)

    def pass_near():
        arrived(0)
        choose()

        @pl.when(c > 0)
        def _():
            near_pair().start()

        @pl.when(c == 0)
        def _():
            last_pair().start()

    def pass_far():
        @pl.when(c < n_ctx - 2)
        def _():
            arrived(1)

        @pl.when(c >= n_ctx - 2)
        def _():
            arrived(0)
            choose()

        last_pair().start()

    def far_grad():
        return remote(hop_g.at[0], hop_g.at[1], hop_send.at[2], hop_recv.at[3], c - mid, h)

    def last_grad(k, j):
        ref = next_in.at[lane_a, lane_rows]
        return remote(hop_g.at[k], ref, hop_send.at[3 + j], ng_recv.at[lane_piece], mid - 1 - j, h)

    def pass_far_grad():
        arrived(2)

        @pl.when(c < n_ctx - 1)
        def _():
            far_grad().start()

        @pl.when(c == n_ctx - 1)
        def _():
            for j in range(2):
                last_grad(0, j).start()

    def pass_near_grad():
        arrived(3)
        last_grad(1, 0).start()

        @pl.when(near)
        def _():
            last_grad(1, 1).start()

        @pl.when(c == mid - 2)
        def _():
            pltpu.make_async_copy(hop_g.at[1], next_in.at[lane_a, lane_rows], ng_recv.at[lane_piece]).start()

    def h_tok(r):
        return peer_of(h, r) * toks

    def in_copy(k, r):
        src, dst = ((q_ref, qb), (g_ref, gb))[k]
        p = peer_of(h, r)
        return remote(src.at[:, cols(p)], dst.at[r], in_send.at[k, r], in_recv.at[k, r], c, p)

    def out_copy(k, r):
        src, dst = ((ob, att_ref), (db, dq_ref))[k]
        p = peer_of(h, r)
        return remote(src.at[r], dst.at[:, cols(h)], out_send.at[k, r], out_recv.at[k, r], c, p)

    barrier = pltpu.get_barrier_semaphore()
    for r in range(1, 8):
        pl.semaphore_signal(barrier, inc=1, device_id=(c, peer_of(h, r)), device_id_type=MESH)
    pl.semaphore_signal(barrier, inc=1, device_id=(mate, h), device_id_type=MESH)

    own_copies = [pltpu.make_async_copy(ref, own.at[a], own_sem.at[a]) for a, ref in enumerate((k_ref, v_ref))]
    own_tiles = [
        pltpu.make_async_copy(ref.at[:, cols(h)], buf.at[0], own_sem.at[2 + a])
        for a, (ref, buf) in enumerate(((q_ref, qb), (g_ref, gb)))
    ]
    for copy in own_copies + own_tiles:
        copy.start()

    def greet(place):
        pl.semaphore_signal(barrier, inc=1, device_id=(place, h), device_id_type=MESH)

    @pl.when(plain)
    def _():
        greet(side)

    def greet_all(places):
        def one(i, carry):
            greet(places(i))
            return carry

        lax.fori_loop(0, mid, one, 0)

    @pl.when(is_high)
    def _():
        greet_all(lambda i: jnp.where(i > 0, i + mid, 0))

    @pl.when(jnp.logical_or(near, c >= n_ctx - 2))
    def _():
        greet(mid - 2)
        greet(mid - 1)

    @pl.when(jnp.logical_and(far, c < n_ctx - 2))
    def _():
        greet(c - mid)

    def count(condition, number):
        return jnp.where(condition, number, 0)

    pl.semaphore_wait(
        barrier, 8 + count(plain, 1) + count(source, mid) + count(jnp.logical_or(near, far), 1)
    )

    for copy in own_copies:
        copy.wait()

    @pl.when(source)
    def _():
        send_parts()

    def send_own(i, carry):
        mate_copy(i, own, part, part_send, part_recv).start()
        return carry

    @pl.when(jnp.logical_not(source))
    def _():
        lax.fori_loop(0, N, send_own, 0)

    def send_in(*tiles):
        for r in tiles:
            for k in range(2):
                in_copy(k, r).start()

    send_in(1, 7, 6)

    @pl.when(jnp.logical_not(near))
    def _():
        send_in(3, 2)

    @pl.when(source)
    def _():
        remote(own, part, src_send.at[0], hop_recv.at[0], mid, h).wait_send()
        lax.fori_loop(0, N, send_own, 0)

    flip_all = jnp.full((PIECE, HD), owner_ref[c], jnp.int32) != c
    n_low = jnp.sum((img_ref[...] < c).astype(jnp.int32), axis=1, keepdims=True)

    def set_half(a, rows, upper, value):
        for b, (both, both_t) in enumerate(((kk, kkt), (vv, vvt))):

            @pl.when(a == b)
            def _():
                cut = slice(HD, None) if upper else slice(0, HD)
                both[rows, cut] = value.astype(BF16)
                both_t[cut, rows] = jnp.transpose(value).astype(BF16)

    near_turn = jnp.maximum(N - 2 - lane_piece, 0)
    late_turn = jnp.where(near, jnp.maximum(near_turn, LATE), LATE)
    far_turn = jnp.minimum(N - 1 - lax.div(lane_piece - 3 + 8, 2) + 4, N - 1)

    def take(i, carry):
        a, rows = piece(i)
        mate_copy(i, own, part, part_send, part_recv).wait_recv()
        mine = own[a, rows].astype(F32)
        other = part[a, rows].astype(F32)
        upper = jnp.where(flip_all, other, mine)

        @pl.when(odd)
        def _():
            fwd[a, rows] = upper.astype(BF16)

            @pl.when(gives)
            def _():
                side_copy(i, fwd, low, fwd_send, fwd_recv).start()

            set_half(a, rows, False, jnp.where(flip_all, mine, other))

        set_half(a, rows, True, upper)

        @pl.when(jnp.logical_and(near, i == near_turn))
        def _():
            pass_near()
            send_in(3, 2)

        @pl.when(i == late_turn)
        def _():
            send_in(5, 4)

        @pl.when(jnp.logical_and(far, i == far_turn))
        def _():
            pass_far()

        return carry

    lax.fori_loop(0, N, take, 0)

    @pl.when(even)
    def _():
        @pl.when(jnp.logical_not(takes))
        def _():
            low[...] = jnp.zeros_like(low)

        def arrive(i, carry):
            a, rows = piece(i)

            @pl.when(jnp.logical_and(takes, jnp.logical_not(is_high)))
            def _():
                side_copy(i, fwd, low, fwd_send, fwd_recv).wait_recv()

            @pl.when(is_high)
            def _():
                remote(low.at[a, rows], low.at[a, rows], hop_send.at[0], cand_recv.at[i], mid, h).wait_recv()

            set_half(a, rows, False, low[a, rows].astype(F32))
            return carry

        lax.fori_loop(0, N, arrive, 0)

    def step(i, carry):
        t = jnp.where(i == 0, 0, jnp.where(i == 1, 3, i - 1))
        r = 2 * t

        @pl.when(t == 0)
        def _():
            for copy in own_tiles:
                copy.wait()

        @pl.when(t > 0)
        def _():
            for k in range(2):
                in_copy(k, r).wait_recv()

        for k in range(2):
            in_copy(k, r + 1).wait_recv()

        @pl.when(jnp.logical_and(i == 3, jnp.logical_not(is_high)))
        def _():
            for r_out in (7, 6, 3, 2):
                for k in range(2):
                    out_copy(k, r_out).start()

        att, dq = pair_step(
            (qb[r], qb[r + 1]),
            (gb[r], gb[r + 1]),
            (h_tok(r), h_tok(r + 1)),
            n_low,
            kk,
            vv,
            kkt,
            vvt,
            ps.at[t],
            dss.at[t],
            qs.at[t],
            gs.at[t],
        )
        for j in range(2):
            ob[r + j] = att[j]
            db[r + j] = dq[j]

        @pl.when(t == 0)
        def _():
            for a, (buf, ref) in enumerate(((ob, att_ref), (db, dq_ref))):
                pltpu.make_async_copy(buf.at[0], ref.at[:, cols(h)], loc_sem.at[a]).start()
            for k in range(2):
                out_copy(k, 1).start()

        @pl.when(jnp.logical_or(i == 3, jnp.logical_and(is_high, i > 0)))
        def _():
            for j in (1, 0):
                for k in range(2):
                    out_copy(k, r + j).start()

        return carry

    lax.fori_loop(0, 4, step, 0)

    for a, (left, right) in enumerate(((dss, qs), (ps, gs))):

        def sums(j, carry):
            i = a * PIECES + j
            rows = pl.ds(pl.multiple_of(j * PIECE, PIECE), PIECE)
            both = summed(left, right, rows)
            tot[...] = both * FACTOR if a == 0 else both

            @pl.when(even)
            def _():
                prev_g[a, rows] = tot[:, :HD].astype(BF16)
                give_grad(i)
                part_g[a, rows] = tot[:, HD:].astype(BF16)
                mate_copy(i, part_g, part_in, pg_send, pg_recv).start()
                fin[a, rows] = tot[:, HD:]

            @pl.when(odd)
            def _():
                @pl.when(gives)
                def _():
                    side_copy(i, prev_g, next_in, ng_send, ng_recv).wait_recv()
                    tot[:, HD:] += next_in[a, rows].astype(F32)

                lower = tot[:, :HD]
                upper = tot[:, HD:]
                part_g[a, rows] = jnp.where(flip_all, upper, lower).astype(BF16)
                mate_copy(i, part_g, part_in, pg_send, pg_recv).start()

                @pl.when(jnp.logical_and(far, i == FAR_GRAD))
                def _():
                    pass_far_grad()

                @pl.when(jnp.logical_and(near, i == NEAR_GRAD))
                def _():
                    pass_near_grad()

                mate_copy(i, part_g, part_in, pg_send, pg_recv).wait_recv()
                other = part_in[a, rows].astype(F32)
                fin[a, rows] = jnp.where(flip_all, lower + other, upper)

            return carry

        lax.fori_loop(0, PIECES, sums, 0)

    @pl.when(even)
    def _():
        @pl.when(far)
        def _():
            pass_far_grad()

        @pl.when(c < mid - 1)
        def _():
            pass_near_grad()

        def finish(i, carry):
            a, rows = piece(i)
            mate_copy(i, part_g, part_in, pg_send, pg_recv).wait_recv()
            other = part_in[a, rows].astype(F32)
            fin[a, rows] = jnp.where(flip_all, other, fin[a, rows] + other)
            return carry

        lax.fori_loop(0, N, finish, 0)

    @pl.when(source)
    def _():
        mine = flip_all == (jnp.full((PIECE, HD), c, jnp.int32) == mid - 2)

        def finish(i, carry):
            a, rows = piece(i)
            remote(next_in.at[a, rows], next_in.at[a, rows], hop_send.at[0], ng_recv.at[i], mid, h).wait_recv()
            other = next_in[a, rows].astype(F32)
            fin[a, rows] += jnp.where(mine, other, jnp.zeros_like(other))
            return carry

        lax.fori_loop(0, N, finish, 0)

    outs = [pltpu.make_async_copy(fin.at[a], ref, loc_sem.at[2 + a]) for a, ref in enumerate((dk_ref, dv_ref))]
    for copy in outs:
        copy.start()

    def drain(i, carry):
        for k in range(2):
            in_copy(k, i).wait_send()
            out_copy(k, i).wait()
        return carry

    lax.fori_loop(1, 8, drain, 0)

    def drain_pieces(i, carry):
        mate_copy(i, own, part, part_send, part_recv).wait_send()
        mate_copy(i, part_g, part_in, pg_send, pg_recv).wait_send()

        @pl.when(gives)
        def _():
            side_copy(i, fwd, low, fwd_send, fwd_recv).wait_send()

        @pl.when(takes)
        def _():
            side_copy(i, prev_g, next_in, ng_send, ng_recv).wait_send()

        return carry

    lax.fori_loop(0, N, drain_pieces, 0)

    @pl.when(jnp.logical_and(near, c > 0))
    def _():
        near_pair().wait_send()

    @pl.when(jnp.logical_or(c == 0, far))
    def _():
        last_pair().wait_send()

    @pl.when(c < mid - 1)
    def _():
        last_grad(1, 0).wait_send()

    @pl.when(jnp.logical_or(near, c == n_ctx - 1))
    def _():
        last_grad(1, 1).wait_send()

    @pl.when(far)
    def _():
        @pl.when(c < n_ctx - 1)
        def _():
            far_grad().wait_send()

        @pl.when(c == n_ctx - 1)
        def _():
            last_grad(0, 0).wait_send()

    for a, (buf, ref) in enumerate(((ob, att_ref), (db, dq_ref))):
        pltpu.make_async_copy(buf.at[0], ref.at[:, cols(h)], loc_sem.at[a]).wait()
    for copy in outs:
        copy.wait()


def store(*refs):
    sources, targets, held, (in_sem, out_sem) = refs[:4], refs[4:8], refs[8:12], refs[12:]

    def copies(j, k):
        size = sources[j].shape[0] // CHUNKS
        rows = pl.ds(k * size, size)
        return (
            pltpu.make_async_copy(sources[j].at[rows], held[j].at[rows], in_sem.at[j, k]),
            pltpu.make_async_copy(held[j].at[rows], targets[j].at[rows], out_sem.at[j, k]),
        )

    every = [copies(j, k) for k in range(CHUNKS) for j in range(4)]
    for inward, _ in every:
        inward.start()
    for inward, outward in every:
        inward.wait()
        outward.start()
    for _, outward in every:
        outward.wait()


def per_device(n_ctx, query, d_out, keys_img, values_img, image_of, owner):
    toks = query.shape[0]
    anywhere = pl.BlockSpec(memory_space=pl.ANY)
    tile = pltpu.VMEM((8, toks, COLS), BF16)
    pair = pltpu.VMEM((2, ROWS, HD), BF16)
    part_rows = PIECE * N // (n_ctx // 2)
    dma = pltpu.SemaphoreType.DMA
    results = pl.pallas_call(
        functools.partial(kernel, n_ctx),
        out_shape=(
            jax.ShapeDtypeStruct(query.shape, BF16),
            jax.ShapeDtypeStruct(query.shape, BF16),
            jax.ShapeDtypeStruct(keys_img.shape, F32),
            jax.ShapeDtypeStruct(values_img.shape, F32),
        ),
        in_specs=[anywhere] * 4
        + [pl.BlockSpec(memory_space=pltpu.VMEM), pl.BlockSpec(memory_space=pltpu.SMEM)],
        out_specs=(anywhere,) * 4,
        scratch_shapes=[tile] * 4
        + [pair] * 4
        + [pltpu.VMEM((ROWS, 2 * HD), BF16)] * 2
        + [pltpu.VMEM((2 * HD, ROWS), BF16)] * 2
        + [pltpu.VMEM((4, ROWS, 2 * GROUP * toks), BF16)] * 2
        + [pltpu.VMEM((4, 2 * GROUP * toks, 2 * HD), BF16)] * 2
        + [pair] * 4
        + [pltpu.VMEM((2, ROWS, HD), F32)]
        + [pltpu.VMEM((PIECE, 2 * HD), F32)]
        + [dma((4,))]
        + [dma((2, 8))] * 4
        + [dma((N,))] * 8
        + [dma((4,))]
        + [pltpu.VMEM((2, part_rows, HD), BF16), pltpu.VMEM((part_rows, HD), BF16), pltpu.VMEM((2, part_rows, HD), BF16)]
        + [dma((5,)), dma((4,)), dma((N,)), dma((1,))],
        compiler_params=pltpu.CompilerParams(collective_id=0, has_side_effects=True, vmem_limit_bytes=60 << 20),
        name="attend",
    )(query, d_out, keys_img, values_img, image_of.reshape(1, -1), owner)
    return pl.pallas_call(
        store,
        out_shape=[jax.ShapeDtypeStruct(x.shape, x.dtype) for x in results],
        in_specs=[anywhere] * 4,
        out_specs=[anywhere] * 4,
        scratch_shapes=[pltpu.VMEM(x.shape, x.dtype) for x in results] + [dma((4, CHUNKS))] * 2,
        name="store",
    )(*results)


def solution(mesh):
    placed = (
        P(("ctx", "head"), None),
        P(("ctx", "head"), None),
        P("ctx", "head"),
        P("ctx", "head"),
        P("ctx"),
        P(),
    )
    return jax.shard_map(
        functools.partial(per_device, mesh.shape["ctx"]),
        mesh=mesh,
        in_specs=placed,
        out_specs=(
            P(("ctx", "head"), None),
            P(("ctx", "head"), None),
            P("ctx", "head"),
            P("ctx", "head"),
        ),
        check_vma=False,
    )
```

```python
import functools

import jax
import jax.numpy as jnp
from jax import lax
from jax.experimental import pallas as pl
from jax.experimental.pallas import tpu as pltpu
from jax.sharding import PartitionSpec as P

HD = 128
GROUP = 8
COLS = GROUP * HD
ROWS = 1024
PIECE = 256
PIECES = ROWS // PIECE
N = 2 * PIECES
FACTOR = HD**-0.5
LOG2E = 1.4426950408889634
CHUNKS = 2
LATE = 5
FAR_GRAD, NEAR_GRAD = 3, 7
MESH = pl.DeviceIdType.MESH
BF16 = jnp.bfloat16
F32 = jnp.float32


def peer_of(h, r):
    b0 = lax.rem(h + r, 2)
    b1 = lax.rem(lax.div(h, 2) + lax.div(r, 2), 2)
    b2 = lax.rem(lax.div(h, 4) + lax.div(r, 4), 2)
    return b0 + 2 * b1 + 4 * b2


def stacked(tile):
    return jnp.concatenate([tile[:, j * HD : (j + 1) * HD] for j in range(GROUP)], axis=0)


def unstacked(rows, toks):
    return jnp.concatenate([rows[j * toks : (j + 1) * toks] for j in range(GROUP)], axis=1)


def pair_step(q_tiles, g_tiles, firsts, n_low, kk, vv, kkt, vvt, p_ref, ds_ref, qs_ref, gs_ref):
    toks = q_tiles[0].shape[0]
    each = toks * GROUP
    rows = 2 * each
    q2 = jnp.concatenate([stacked(tile) for tile in q_tiles], axis=0).astype(F32)
    g2 = jnp.concatenate([stacked(tile) for tile in g_tiles], axis=0).astype(F32)

    def is_low(shape, axis):
        at = lax.broadcasted_iota(jnp.int32, shape, axis)
        return lax.rem(at, toks) + jnp.where(at < each, firsts[0], firsts[1]) < n_low

    low_lane = is_low((HD, rows), 1)
    low_row = is_low((rows, HD), 0)

    def halves(x, mask, axis):
        zero = jnp.zeros_like(x)
        return jnp.concatenate([jnp.where(mask, x, zero), jnp.where(mask, zero, x)], axis=axis).astype(BF16)

    qt = jnp.transpose(q2)
    gt = jnp.transpose(g2)
    st = jnp.dot(kk[...], halves(qt, low_lane, 0), preferred_element_type=F32)
    top = jnp.max(st, axis=0, keepdims=True)
    ex = jnp.exp2((st - top) * (FACTOR * LOG2E))
    inv = 1.0 / jnp.sum(ex, axis=0, keepdims=True)
    p = ex.astype(BF16)
    p_ref[...] = p
    inv_row = jnp.transpose(jnp.broadcast_to(inv, (HD, rows)))
    qs_ref[...] = halves(q2 * inv_row, low_row, 1)
    gs_ref[...] = halves(g2 * inv_row, low_row, 1)
    ot = jnp.dot(vvt[...], p, preferred_element_type=F32)
    ot = (jnp.where(low_lane, ot[:HD], ot[HD:]) * inv).astype(BF16).astype(F32)
    delta = jnp.sum(gt * ot, axis=0, keepdims=True)
    dp = jnp.dot(vv[...], halves(gt, low_lane, 0), preferred_element_type=F32)
    ds = (p.astype(F32) * (dp - delta)).astype(BF16)
    ds_ref[...] = ds
    dqt = jnp.dot(kkt[...], ds, preferred_element_type=F32)
    dqt = jnp.where(low_lane, dqt[:HD], dqt[HD:]) * (inv * FACTOR)
    att = jnp.transpose(ot).astype(BF16)
    dq = jnp.transpose(dqt).astype(BF16)
    return (
        [unstacked(att[:each], toks), unstacked(att[each:], toks)],
        [unstacked(dq[:each], toks), unstacked(dq[each:], toks)],
    )


def summed(left, right, rows):
    total = jnp.dot(left[0, rows], right[0], preferred_element_type=F32)
    for t in range(1, left.shape[0]):
        total = total + jnp.dot(left[t, rows], right[t], preferred_element_type=F32)
    return total


def kernel(
    n_ctx,
    q_ref,
    g_ref,
    k_ref,
    v_ref,
    img_ref,
    owner_ref,
    att_ref,
    dq_ref,
    dk_ref,
    dv_ref,
    qb,
    gb,
    ob,
    db,
    own,
    part,
    low,
    fwd,
    kk,
    vv,
    kkt,
    vvt,
    ps,
    dss,
    qs,
    gs,
    part_g,
    prev_g,
    part_in,
    next_in,
    fin,
    tot,
    own_sem,
    in_send,
    in_recv,
    out_send,
    out_recv,
    part_send,
    part_recv,
    fwd_send,
    fwd_recv,
    pg_send,
    pg_recv,
    ng_send,
    ng_recv,
    loc_sem,
    hop,
    chosen,
    hop_g,
    hop_send,
    hop_recv,
    cand_recv,
    src_send,
):
    c = lax.axis_index("ctx")
    h = lax.axis_index("head")
    toks = qb.shape[1]
    odd = lax.rem(c, 2) == 1
    even = lax.rem(c, 2) == 0
    mate = c + 1 - 2 * lax.rem(c, 2)
    side = lax.rem(c + 2 * lax.rem(c, 2) - 1 + n_ctx, n_ctx)
    has_side = jnp.logical_and(c > 0, c < n_ctx - 1)
    mid = n_ctx // 2
    subs = mid // N
    lane = lax.rem(c, mid)
    lane_piece = lax.div(lane, subs)
    is_low = c == mid - 1
    is_high = c == mid
    source = jnp.logical_or(is_low, c == mid - 2)
    near = c < mid - 2
    far = c > mid
    plain = jnp.logical_and(has_side, jnp.logical_not(jnp.logical_or(is_low, is_high)))
    gives = jnp.logical_and(jnp.logical_and(odd, c < n_ctx - 1), jnp.logical_not(is_low))
    takes = jnp.logical_and(even, c > 0)

    def cols(p):
        return pl.ds(pl.multiple_of(p * COLS, COLS), COLS)

    def piece(i):
        return lax.div(i, PIECES), pl.ds(pl.multiple_of(lax.rem(i, PIECES) * PIECE, PIECE), PIECE)

    def remote(src, dst, send, recv, place, head):
        return pltpu.make_async_remote_copy(
            src_ref=src, dst_ref=dst, send_sem=send, recv_sem=recv, device_id=(place, head), device_id_type=MESH
        )

    def mate_copy(i, src, dst, send, recv):
        a, rows = piece(i)
        return remote(src.at[a, rows], dst.at[a, rows], send.at[i], recv.at[i], mate, h)

    def side_copy(i, src, dst, send, recv):
        a, rows = piece(i)
        return remote(src.at[a, rows], dst.at[a, rows], send.at[i], recv.at[i], side, h)

    def part_of(i):
        a = lax.div(i, subs * PIECES)
        return a, pl.ds(pl.multiple_of(lax.rem(i, subs * PIECES) * (PIECE // subs), PIECE // subs), PIECE // subs)

    def send_parts():
        at = c - (mid - 2)

        def one(i, carry):
            a, rows = part_of(i)

            @pl.when(i < mid - 2)
            def _():
                remote(own.at[a, rows], hop.at[at], src_send.at[0], hop_recv.at[0], i, h).start()

            @pl.when(i >= mid - 2)
            def _():
                remote(own.at[a, rows], hop.at[at], src_send.at[0], hop_recv.at[0], mid + i, h).start()

            return carry

        lax.fori_loop(0, mid, one, 0)

    def give_grad(i):
        @pl.when(jnp.logical_and(takes, jnp.logical_not(is_high)))
        def _():
            side_copy(i, prev_g, next_in, ng_send, ng_recv).start()

        @pl.when(is_high)
        def _():
            for j in range(subs):
                to = i * subs + j
                a, rows = part_of(to)

                @pl.when(to > 0)
                def _():
                    remote(prev_g.at[a, rows], hop_g.at[0], ng_send.at[i], hop_recv.at[2], mid + to, h).start()

                @pl.when(to == 0)
                def _():
                    remote(prev_g.at[a, rows], hop_g.at[1], ng_send.at[i], hop_recv.at[3], 0, h).start()

    lane_a, lane_rows = part_of(lane)

    def arrived(k):
        ref = hop if k == 0 else chosen if k == 1 else hop_g.at[k - 2]
        remote(ref, ref, hop_send.at[0], hop_recv.at[k], mid, h).wait_recv()

    def choose():
        flipped = jnp.full(chosen.shape, owner_ref[mid - 1], jnp.int32) != mid - 1
        chosen[...] = jnp.where(flipped, hop[0].astype(F32), hop[1].astype(F32)).astype(BF16)

    def near_pair():
        return remote(chosen, chosen, hop_send.at[0], hop_recv.at[1], c + mid, h)

    def last_pair():
        return remote(chosen, low.at[lane_a, lane_rows], hop_send.at[1], cand_recv.at[lane_piece], mid, h)

    def pass_near():
        arrived(0)
        choose()

        @pl.when(c > 0)
        def _():
            near_pair().start()

        @pl.when(c == 0)
        def _():
            last_pair().start()

    def pass_far():
        @pl.when(c < n_ctx - 2)
        def _():
            arrived(1)

        @pl.when(c >= n_ctx - 2)
        def _():
            arrived(0)
            choose()

        last_pair().start()

    def far_grad():
        return remote(hop_g.at[0], hop_g.at[1], hop_send.at[2], hop_recv.at[3], c - mid, h)

    def last_grad(k, j):
        ref = next_in.at[lane_a, lane_rows]
        return remote(hop_g.at[k], ref, hop_send.at[3 + j], ng_recv.at[lane_piece], mid - 1 - j, h)

    def pass_far_grad():
        arrived(2)

        @pl.when(c < n_ctx - 1)
        def _():
            far_grad().start()

        @pl.when(c == n_ctx - 1)
        def _():
            for j in range(2):
                last_grad(0, j).start()

    def pass_near_grad():
        arrived(3)
        last_grad(1, 0).start()

        @pl.when(near)
        def _():
            last_grad(1, 1).start()

        @pl.when(c == mid - 2)
        def _():
            pltpu.make_async_copy(hop_g.at[1], next_in.at[lane_a, lane_rows], ng_recv.at[lane_piece]).start()

    def h_tok(r):
        return peer_of(h, r) * toks

    def in_copy(k, r):
        src, dst = ((q_ref, qb), (g_ref, gb))[k]
        p = peer_of(h, r)
        return remote(src.at[:, cols(p)], dst.at[r], in_send.at[k, r], in_recv.at[k, r], c, p)

    def out_copy(k, r):
        src, dst = ((ob, att_ref), (db, dq_ref))[k]
        p = peer_of(h, r)
        return remote(src.at[r], dst.at[:, cols(h)], out_send.at[k, r], out_recv.at[k, r], c, p)

    barrier = pltpu.get_barrier_semaphore()
    for r in range(1, 8):
        pl.semaphore_signal(barrier, inc=1, device_id=(c, peer_of(h, r)), device_id_type=MESH)
    pl.semaphore_signal(barrier, inc=1, device_id=(mate, h), device_id_type=MESH)

    own_copies = [pltpu.make_async_copy(ref, own.at[a], own_sem.at[a]) for a, ref in enumerate((k_ref, v_ref))]
    own_tiles = [
        pltpu.make_async_copy(ref.at[:, cols(h)], buf.at[0], own_sem.at[2 + a])
        for a, (ref, buf) in enumerate(((q_ref, qb), (g_ref, gb)))
    ]
    for copy in own_copies + own_tiles:
        copy.start()

    def greet(place):
        pl.semaphore_signal(barrier, inc=1, device_id=(place, h), device_id_type=MESH)

    @pl.when(plain)
    def _():
        greet(side)

    def greet_all(places):
        def one(i, carry):
            greet(places(i))
            return carry

        lax.fori_loop(0, mid, one, 0)

    @pl.when(is_high)
    def _():
        greet_all(lambda i: jnp.where(i > 0, i + mid, 0))

    @pl.when(jnp.logical_or(near, c >= n_ctx - 2))
    def _():
        greet(mid - 2)
        greet(mid - 1)

    @pl.when(jnp.logical_and(far, c < n_ctx - 2))
    def _():
        greet(c - mid)

    def count(condition, number):
        return jnp.where(condition, number, 0)

    pl.semaphore_wait(
        barrier, 8 + count(plain, 1) + count(source, mid) + count(jnp.logical_or(near, far), 1)
    )

    for copy in own_copies:
        copy.wait()

    @pl.when(source)
    def _():
        send_parts()

    def send_own(i, carry):
        mate_copy(i, own, part, part_send, part_recv).start()
        return carry

    @pl.when(jnp.logical_not(source))
    def _():
        lax.fori_loop(0, N, send_own, 0)

    def send_in(*tiles):
        for r in tiles:
            for k in range(2):
                in_copy(k, r).start()

    send_in(1, 7, 6)

    @pl.when(jnp.logical_not(near))
    def _():
        send_in(3, 2)

    @pl.when(source)
    def _():
        remote(own, part, src_send.at[0], hop_recv.at[0], mid, h).wait_send()
        lax.fori_loop(0, N, send_own, 0)

    flip_all = jnp.full((PIECE, HD), owner_ref[c], jnp.int32) != c
    n_low = jnp.sum((img_ref[...] < c).astype(jnp.int32), axis=1, keepdims=True)

    def set_half(a, rows, upper, value):
        for b, (both, both_t) in enumerate(((kk, kkt), (vv, vvt))):

            @pl.when(a == b)
            def _():
                cut = slice(HD, None) if upper else slice(0, HD)
                both[rows, cut] = value.astype(BF16)
                both_t[cut, rows] = jnp.transpose(value).astype(BF16)

    near_turn = jnp.maximum(N - 3 - lane_piece, 0)
    late_turn = jnp.where(near, jnp.maximum(near_turn, LATE), LATE)
    far_turn = jnp.minimum(N - 1 - lax.div(lane_piece - 3 + 8, 2) + 4, N - 1)

    def take(i, carry):
        a, rows = piece(i)
        mate_copy(i, own, part, part_send, part_recv).wait_recv()
        mine = own[a, rows].astype(F32)
        other = part[a, rows].astype(F32)
        upper = jnp.where(flip_all, other, mine)

        @pl.when(odd)
        def _():
            fwd[a, rows] = upper.astype(BF16)

            @pl.when(gives)
            def _():
                side_copy(i, fwd, low, fwd_send, fwd_recv).start()

            set_half(a, rows, False, jnp.where(flip_all, mine, other))

        set_half(a, rows, True, upper)

        @pl.when(jnp.logical_and(near, i == near_turn))
        def _():
            pass_near()
            send_in(3, 2)

        @pl.when(i == late_turn)
        def _():
            send_in(5, 4)

        @pl.when(jnp.logical_and(far, i == far_turn))
        def _():
            pass_far()

        return carry

    lax.fori_loop(0, N, take, 0)

    @pl.when(even)
    def _():
        @pl.when(jnp.logical_not(takes))
        def _():
            low[...] = jnp.zeros_like(low)

        def arrive(i, carry):
            a, rows = piece(i)

            @pl.when(jnp.logical_and(takes, jnp.logical_not(is_high)))
            def _():
                side_copy(i, fwd, low, fwd_send, fwd_recv).wait_recv()

            @pl.when(is_high)
            def _():
                remote(low.at[a, rows], low.at[a, rows], hop_send.at[0], cand_recv.at[i], mid, h).wait_recv()

            set_half(a, rows, False, low[a, rows].astype(F32))
            return carry

        lax.fori_loop(0, N, arrive, 0)

    def step(i, carry):
        t = jnp.where(i == 0, 0, jnp.where(i == 1, 3, i - 1))
        r = 2 * t

        @pl.when(t == 0)
        def _():
            for copy in own_tiles:
                copy.wait()

        @pl.when(t > 0)
        def _():
            for k in range(2):
                in_copy(k, r).wait_recv()

        for k in range(2):
            in_copy(k, r + 1).wait_recv()

        @pl.when(jnp.logical_and(i == 3, jnp.logical_not(is_high)))
        def _():
            for r_out in (7, 6, 3, 2):
                for k in range(2):
                    out_copy(k, r_out).start()

        att, dq = pair_step(
            (qb[r], qb[r + 1]),
            (gb[r], gb[r + 1]),
            (h_tok(r), h_tok(r + 1)),
            n_low,
            kk,
            vv,
            kkt,
            vvt,
            ps.at[t],
            dss.at[t],
            qs.at[t],
            gs.at[t],
        )
        for j in range(2):
            ob[r + j] = att[j]
            db[r + j] = dq[j]

        @pl.when(t == 0)
        def _():
            for a, (buf, ref) in enumerate(((ob, att_ref), (db, dq_ref))):
                pltpu.make_async_copy(buf.at[0], ref.at[:, cols(h)], loc_sem.at[a]).start()
            for k in range(2):
                out_copy(k, 1).start()

        @pl.when(jnp.logical_or(i == 3, jnp.logical_and(is_high, i > 0)))
        def _():
            for j in (1, 0):
                for k in range(2):
                    out_copy(k, r + j).start()

        return carry

    lax.fori_loop(0, 4, step, 0)

    for a, (left, right) in enumerate(((dss, qs), (ps, gs))):

        def sums(j, carry):
            i = a * PIECES + j
            rows = pl.ds(pl.multiple_of(j * PIECE, PIECE), PIECE)
            both = summed(left, right, rows)
            tot[...] = both * FACTOR if a == 0 else both

            @pl.when(even)
            def _():
                prev_g[a, rows] = tot[:, :HD].astype(BF16)
                give_grad(i)
                part_g[a, rows] = tot[:, HD:].astype(BF16)
                mate_copy(i, part_g, part_in, pg_send, pg_recv).start()
                fin[a, rows] = tot[:, HD:]

            @pl.when(odd)
            def _():
                @pl.when(gives)
                def _():
                    side_copy(i, prev_g, next_in, ng_send, ng_recv).wait_recv()
                    tot[:, HD:] += next_in[a, rows].astype(F32)

                lower = tot[:, :HD]
                upper = tot[:, HD:]
                part_g[a, rows] = jnp.where(flip_all, upper, lower).astype(BF16)
                mate_copy(i, part_g, part_in, pg_send, pg_recv).start()

                @pl.when(jnp.logical_and(far, i == FAR_GRAD))
                def _():
                    pass_far_grad()

                @pl.when(jnp.logical_and(near, i == NEAR_GRAD))
                def _():
                    pass_near_grad()

                mate_copy(i, part_g, part_in, pg_send, pg_recv).wait_recv()
                other = part_in[a, rows].astype(F32)
                fin[a, rows] = jnp.where(flip_all, lower + other, upper)

            return carry

        lax.fori_loop(0, PIECES, sums, 0)

    @pl.when(even)
    def _():
        @pl.when(far)
        def _():
            pass_far_grad()

        @pl.when(c < mid - 1)
        def _():
            pass_near_grad()

        def finish(i, carry):
            a, rows = piece(i)
            mate_copy(i, part_g, part_in, pg_send, pg_recv).wait_recv()
            other = part_in[a, rows].astype(F32)
            fin[a, rows] = jnp.where(flip_all, other, fin[a, rows] + other)
            return carry

        lax.fori_loop(0, N, finish, 0)

    @pl.when(source)
    def _():
        mine = flip_all == (jnp.full((PIECE, HD), c, jnp.int32) == mid - 2)

        def finish(i, carry):
            a, rows = piece(i)
            remote(next_in.at[a, rows], next_in.at[a, rows], hop_send.at[0], ng_recv.at[i], mid, h).wait_recv()
            other = next_in[a, rows].astype(F32)
            fin[a, rows] += jnp.where(mine, other, jnp.zeros_like(other))
            return carry

        lax.fori_loop(0, N, finish, 0)

    outs = [pltpu.make_async_copy(fin.at[a], ref, loc_sem.at[2 + a]) for a, ref in enumerate((dk_ref, dv_ref))]
    for copy in outs:
        copy.start()

    def drain(i, carry):
        for k in range(2):
            in_copy(k, i).wait_send()
            out_copy(k, i).wait()
        return carry

    lax.fori_loop(1, 8, drain, 0)

    def drain_pieces(i, carry):
        mate_copy(i, own, part, part_send, part_recv).wait_send()
        mate_copy(i, part_g, part_in, pg_send, pg_recv).wait_send()

        @pl.when(gives)
        def _():
            side_copy(i, fwd, low, fwd_send, fwd_recv).wait_send()

        @pl.when(takes)
        def _():
            side_copy(i, prev_g, next_in, ng_send, ng_recv).wait_send()

        return carry

    lax.fori_loop(0, N, drain_pieces, 0)

    @pl.when(jnp.logical_and(near, c > 0))
    def _():
        near_pair().wait_send()

    @pl.when(jnp.logical_or(c == 0, far))
    def _():
        last_pair().wait_send()

    @pl.when(c < mid - 1)
    def _():
        last_grad(1, 0).wait_send()

    @pl.when(jnp.logical_or(near, c == n_ctx - 1))
    def _():
        last_grad(1, 1).wait_send()

    @pl.when(far)
    def _():
        @pl.when(c < n_ctx - 1)
        def _():
            far_grad().wait_send()

        @pl.when(c == n_ctx - 1)
        def _():
            last_grad(0, 0).wait_send()

    for a, (buf, ref) in enumerate(((ob, att_ref), (db, dq_ref))):
        pltpu.make_async_copy(buf.at[0], ref.at[:, cols(h)], loc_sem.at[a]).wait()
    for copy in outs:
        copy.wait()


def store(*refs):
    sources, targets, held, (in_sem, out_sem) = refs[:4], refs[4:8], refs[8:12], refs[12:]

    def copies(j, k):
        size = sources[j].shape[0] // CHUNKS
        rows = pl.ds(k * size, size)
        return (
            pltpu.make_async_copy(sources[j].at[rows], held[j].at[rows], in_sem.at[j, k]),
            pltpu.make_async_copy(held[j].at[rows], targets[j].at[rows], out_sem.at[j, k]),
        )

    every = [copies(j, k) for k in range(CHUNKS) for j in range(4)]
    for inward, _ in every:
        inward.start()
    for inward, outward in every:
        inward.wait()
        outward.start()
    for _, outward in every:
        outward.wait()


def per_device(n_ctx, query, d_out, keys_img, values_img, image_of, owner):
    toks = query.shape[0]
    anywhere = pl.BlockSpec(memory_space=pl.ANY)
    tile = pltpu.VMEM((8, toks, COLS), BF16)
    pair = pltpu.VMEM((2, ROWS, HD), BF16)
    part_rows = PIECE * N // (n_ctx // 2)
    dma = pltpu.SemaphoreType.DMA
    results = pl.pallas_call(
        functools.partial(kernel, n_ctx),
        out_shape=(
            jax.ShapeDtypeStruct(query.shape, BF16),
            jax.ShapeDtypeStruct(query.shape, BF16),
            jax.ShapeDtypeStruct(keys_img.shape, F32),
            jax.ShapeDtypeStruct(values_img.shape, F32),
        ),
        in_specs=[anywhere] * 4
        + [pl.BlockSpec(memory_space=pltpu.VMEM), pl.BlockSpec(memory_space=pltpu.SMEM)],
        out_specs=(anywhere,) * 4,
        scratch_shapes=[tile] * 4
        + [pair] * 4
        + [pltpu.VMEM((ROWS, 2 * HD), BF16)] * 2
        + [pltpu.VMEM((2 * HD, ROWS), BF16)] * 2
        + [pltpu.VMEM((4, ROWS, 2 * GROUP * toks), BF16)] * 2
        + [pltpu.VMEM((4, 2 * GROUP * toks, 2 * HD), BF16)] * 2
        + [pair] * 4
        + [pltpu.VMEM((2, ROWS, HD), F32)]
        + [pltpu.VMEM((PIECE, 2 * HD), F32)]
        + [dma((4,))]
        + [dma((2, 8))] * 4
        + [dma((N,))] * 8
        + [dma((4,))]
        + [pltpu.VMEM((2, part_rows, HD), BF16), pltpu.VMEM((part_rows, HD), BF16), pltpu.VMEM((2, part_rows, HD), BF16)]
        + [dma((5,)), dma((4,)), dma((N,)), dma((1,))],
        compiler_params=pltpu.CompilerParams(collective_id=0, has_side_effects=True, vmem_limit_bytes=60 << 20),
        name="attend",
    )(query, d_out, keys_img, values_img, image_of.reshape(1, -1), owner)
    return pl.pallas_call(
        store,
        out_shape=[jax.ShapeDtypeStruct(x.shape, x.dtype) for x in results],
        in_specs=[anywhere] * 4,
        out_specs=[anywhere] * 4,
        scratch_shapes=[pltpu.VMEM(x.shape, x.dtype) for x in results] + [dma((4, CHUNKS))] * 2,
        name="store",
    )(*results)


def solution(mesh):
    placed = (
        P(("ctx", "head"), None),
        P(("ctx", "head"), None),
        P("ctx", "head"),
        P("ctx", "head"),
        P("ctx"),
        P(),
    )
    return jax.shard_map(
        functools.partial(per_device, mesh.shape["ctx"]),
        mesh=mesh,
        in_specs=placed,
        out_specs=(
            P(("ctx", "head"), None),
            P(("ctx", "head"), None),
            P("ctx", "head"),
            P("ctx", "head"),
        ),
        check_vma=False,
    )
```
